512 devices in a mesh: dp: 64 (over z_hi, x, y, core), section: 8 (over z_lo).
Axes of the slice: x: 4, y: 4, z: 16 (z_hi: 2, z_lo: 8; z = z_hi * 8 + z_lo), core: 2. Of those that a mesh axis runs over, the one named last changes fastest.
Arguments:
- projections: float32 [2048, 128], P('dp'), may hold values from -2.5 to 2.5
- partner: int32 [2048], P('dp'), may hold values from 0 to 2047, as said below
- plan: int32 [64, 32], P('dp'), may hold values from 0 to 31, as said below
- head_pre: bfloat16 [128, 2048], P('dp', 'section'), may hold values from -6 to 6
- head_in: bfloat16 [512, 2048], P(None, 'section'), may hold values from -0.25 to 0.25
- head_out: bfloat16 [2048, 128], P('section'), may hold values from -0.125 to 0.125
- final_pre: bfloat16 [128, 8, 8, 8, 512], P('dp'), may hold values from -6 to 6
- incoming: bfloat16 [8, 128, 8, 8, 8, 512], P('section', 'dp'), may hold values from -6 to 6
- input_pre: bfloat16 [8, 128, 8, 8, 8, 512], P('section', 'dp'), may hold values from -6 to 6
- mid_pre1: bfloat16 [8, 128, 8, 8, 8, 128], P('section', 'dp'), may hold values from -6 to 6
- mid_pre2: bfloat16 [8, 128, 8, 8, 8, 128], P('section', 'dp'), may hold values from -6 to 6
- w_reduce: bfloat16 [8, 512, 128], P('section', 'dp'), may hold values from -0.25 to 0.25
- w_spatial: bfloat16 [8, 3456, 128], P('section', 'dp'), may hold values from -0.109375 to 0.109375
- w_expand: bfloat16 [8, 128, 512], P('section', 'dp'), may hold values from -0.5 to 0.5
- gain1: float32 [8, 128], P('section'), may hold values from 0.5 to 2
- gain2: float32 [8, 128], P('section'), may hold values from 0.5 to 2
- gain3: float32 [8, 512], P('section'), may hold values from 0.5 to 2
Outputs:
- projection_gradient: float32 [2048, 128], P('dp')
- input_grad: bfloat16 [8, 128, 8, 8, 8, 512], P('section', 'dp')
- grad_reduce: bfloat16 [8, 512, 128], P('section', 'dp')
- grad_spatial: bfloat16 [8, 3456, 128], P('section', 'dp')
- grad_expand: bfloat16 [8, 128, 512], P('section', 'dp')
The draws below stay inside these ranges and needn't reach their ends.
Inputs may be any that keep to these rules, and one draw needn't show every extreme that they name: partner[partner[i]] = i and partner[i] != i for every crop i. `plan`: each row names every number 0 to 31 once; the window's microbatch uses the first 2 entries of each row.
All inputs are finite; a program needn't handle non-finite values.
Results may differ from the reference program's by a relative error of at most 0.009.
Values may be sent and summed in bfloat16 or wider, within the bound.
No kernel may reach another device: no remote copies, remote signals or barrier semaphores. Data moves between devices by JAX's collectives and lax.ppermute only.
A program may use at most 64 MiB of HBM per device.

```python
import math
import jax
import jax.numpy as jnp
from jax import lax

P_SIZE = 128
C = 512
B = 128
HID = 2048
S = 8
MICRO = 2
ROWS = 32
VOX = 512
CROPS = 2048
CROPS_MB = 128
SECTIONS = 8
N_DP = 64


def draw_projections(key, part):
    key = jax.random.fold_in(key, 11)
    base_key = jax.random.fold_in(key, 0)
    values = jnp.clip(jax.random.normal(base_key, (CROPS, P_SIZE), jnp.float32), -6.5, 6.5)
    return 0.36 * values


def draw_partner(key, part):
    key = jax.random.fold_in(key, 23)
    order = jax.random.permutation(key, CROPS).astype(jnp.int32)
    swapped = order.reshape(-1, 2)[:, ::-1].reshape(-1)
    return jnp.zeros((CROPS,), jnp.int32).at[order].set(swapped)


def draw_plan(key, part):
    key = jax.random.fold_in(key, 37)
    group_keys = jax.random.split(key, CROPS // ROWS)

    def one_order(single_key):
        return jax.random.permutation(single_key, ROWS)
    return jax.vmap(one_order)(group_keys).astype(jnp.int32)


def shard_levels(rng, shape, cuts, smallest, high):
    level = 1.0
    for dim, shards_of in cuts:
        draws = jax.random.uniform(jax.random.fold_in(jax.random.fold_in(rng, 6), dim), (shards_of,), jnp.float32, smallest / len(cuts), high / len(cuts))
        level = level * jnp.repeat(jnp.exp(draws), shape[dim] // shards_of).reshape((-1,) + (1,) * (len(shape) - 1 - dim))
    return level


def scatter_about(rng, dims, scale, limit, shards=(), kind=jnp.bfloat16):
    array = scale * jax.random.normal(rng, dims, jnp.float32)
    if shards:
        array = array * shard_levels(rng, dims, shards, -0.22, 0.18)
    return jnp.clip(array, -limit, limit).astype(kind)


def setup_inputs(seed: int = 0) -> dict:
    streams_of = jax.random.split(jax.random.key(seed), 18)
    projections = draw_projections(jax.random.fold_in(streams_of[17], 71), 0)
    partner = draw_partner(jax.random.fold_in(streams_of[17], 71), 0)
    plan = draw_plan(jax.random.fold_in(streams_of[17], 71), 0)
    head_pre = scatter_about(streams_of[3], (CROPS_MB, HID), 1.0, 6.0, ((0, 64), (1, 8)))
    head_in = scatter_about(streams_of[4], (C, HID), C ** -0.5, 0.25, ((1, 8),))
    head_out = scatter_about(streams_of[5], (HID, P_SIZE), HID ** -0.5, 0.125, ((0, 8),))
    final_pre = scatter_about(streams_of[6], (CROPS_MB, S, S, S, C), 1.0, 6.0, ((0, 64),))
    incoming = scatter_about(streams_of[7], (SECTIONS, CROPS_MB, S, S, S, C), 1.0, 6.0, ((0, 8), (1, 64)))
    input_pre = scatter_about(streams_of[8], (SECTIONS, CROPS_MB, S, S, S, C), 1.0, 6.0, ((0, 8), (1, 64)))
    mid_pre1 = scatter_about(streams_of[9], (SECTIONS, CROPS_MB, S, S, S, B), 1.0, 6.0, ((0, 8), (1, 64)))
    mid_pre2 = scatter_about(streams_of[10], (SECTIONS, CROPS_MB, S, S, S, B), 1.0, 6.0, ((0, 8), (1, 64)))
    w_reduce = scatter_about(streams_of[11], (SECTIONS, C, B), C ** -0.5, 0.25, ((0, 8), (1, 64)))
    w_spatial = scatter_about(streams_of[12], (SECTIONS, 27 * B, B), (27 * B) ** -0.5, 0.109375, ((0, 8), (1, 64)))
    w_expand = scatter_about(streams_of[13], (SECTIONS, B, C), B ** -0.5, 0.5, ((0, 8), (1, 64)))
    gain1 = jnp.clip(jnp.exp(math.log(2.0) - 1.3862944 * jax.random.uniform(streams_of[14], (SECTIONS, B), jnp.float32) ** shard_levels(streams_of[14], (SECTIONS, B), ((0, 8),), -0.2, 0.2)), 0.5, 2.0)
    gain2 = jnp.clip(jnp.exp(math.log(2.0) - 1.3862944 * jax.random.uniform(streams_of[15], (SECTIONS, B), jnp.float32) ** shard_levels(streams_of[15], (SECTIONS, B), ((0, 8),), -0.2, 0.2)), 0.5, 2.0)
    gain3 = jnp.clip(jnp.exp(math.log(2.0) - 1.3862944 * jax.random.uniform(streams_of[16], (SECTIONS, C), jnp.float32) ** shard_levels(streams_of[16], (SECTIONS, C), ((0, 8),), -0.2, 0.2)), 0.5, 2.0)
    return dict(projections=projections, partner=partner, plan=plan, head_pre=head_pre, head_in=head_in, head_out=head_out, final_pre=final_pre, incoming=incoming, input_pre=input_pre, mid_pre1=mid_pre1, mid_pre2=mid_pre2, w_reduce=w_reduce, w_spatial=w_spatial, w_expand=w_expand, gain1=gain1, gain2=gain2, gain3=gain3)


SOFTMAX_TEMP = 0.5
LOSS_SCALE = 1024.0


def shifted(volume, off_a, off_b, off_c):
    extent = volume.shape[1]
    padded = jnp.pad(volume, ((0, 0), (1, 1), (1, 1), (1, 1), (0, 0)))
    return padded[:, 1 + off_a:1 + off_a + extent, 1 + off_b:1 + off_b + extent, 1 + off_c:1 + off_c + extent, :]


def block_backward(out_grad, input_pre, mid_pre1, mid_pre2, w_reduce, w_spatial, w_expand, gain1, gain2, gain3, inverse):
    narrow = mid_pre1.shape[-1]
    wide = out_grad.shape[-1]
    e_three = (gain3 * out_grad).astype(jnp.bfloat16)
    flat_three = e_three.reshape(-1, wide)
    hidden_two = jnp.maximum(mid_pre2, 0).astype(jnp.bfloat16)
    grad_expand = jnp.dot(hidden_two.reshape(-1, narrow).T, flat_three, preferred_element_type=jnp.float32) * inverse
    back_two = jnp.dot(flat_three, w_expand.T, preferred_element_type=jnp.float32).reshape(mid_pre2.shape)
    e_two = jnp.where(mid_pre2 > 0, gain2 * back_two, 0.0).astype(jnp.bfloat16)
    flat_two = e_two.reshape(-1, narrow)
    hidden_one = jnp.maximum(mid_pre1, 0).astype(jnp.bfloat16)
    spatial_parts = []
    back_one = jnp.zeros(mid_pre1.shape, jnp.float32)
    for off_a in (-1, 0, 1):
        block_start = (off_a + 1) * 9 * narrow
        columns = jnp.concatenate([shifted(hidden_one, off_a, off_b, off_c) for off_b in (-1, 0, 1) for off_c in (-1, 0, 1)], axis=-1)
        columns = columns.reshape(-1, 9 * narrow)
        spatial_parts.append(jnp.dot(columns.T, flat_two, preferred_element_type=jnp.float32) * inverse)
        spread = jnp.dot(flat_two, w_spatial[block_start:block_start + 9 * narrow].T, preferred_element_type=jnp.float32)
        spread = spread.reshape(mid_pre1.shape[:-1] + (9, narrow))
        for off_b in (-1, 0, 1):
            for off_c in (-1, 0, 1):
                position = 3 * (off_b + 1) + (off_c + 1)
                back_one = back_one + shifted(spread[..., position, :], -off_a, -off_b, -off_c)
    grad_spatial = jnp.concatenate(spatial_parts, axis=0)
    e_one = jnp.where(mid_pre1 > 0, gain1 * back_one, 0.0).astype(jnp.bfloat16)
    flat_one = e_one.reshape(-1, narrow)
    inputs = jnp.maximum(input_pre, 0).astype(jnp.bfloat16)
    grad_reduce = jnp.dot(inputs.reshape(-1, wide).T, flat_one, preferred_element_type=jnp.float32) * inverse
    through = jnp.dot(flat_one, w_reduce.T, preferred_element_type=jnp.float32).reshape(out_grad.shape)
    input_grad = jnp.where(input_pre > 0, through + out_grad, 0.0).astype(jnp.bfloat16)
    return input_grad, grad_reduce, grad_spatial, grad_expand


def reference(projections, partner, plan, head_pre, head_in, head_out, final_pre, incoming, input_pre, mid_pre1, mid_pre2, w_reduce, w_spatial, w_expand, gain1, gain2, gain3):
    row_peak = lax.Precision.HIGHEST
    similarity_scores = jnp.dot(projections, projections.T, precision=row_peak) / SOFTMAX_TEMP
    crop_count = similarity_scores.shape[0]
    diagonal = jnp.eye(crop_count, dtype=bool)
    masked = jnp.where(diagonal, -jnp.inf, similarity_scores)
    largest = jnp.max(masked, axis=1, keepdims=True)
    totals = largest + jnp.log(jnp.sum(jnp.exp(masked - largest), axis=1, keepdims=True))
    prob = jnp.exp(masked - totals)
    blended_terms = prob + prob.T
    projection_gradient = (jnp.dot(blended_terms, projections, precision=row_peak) - 2.0 * projections[partner]) / SOFTMAX_TEMP
    group_count = plan.shape[0]
    per_group = crop_count // group_count
    picked = (jnp.arange(group_count, dtype=jnp.int32)[:, None] * per_group + plan[:, :MICRO]).reshape(-1).astype(jnp.int32)
    mb_grad = projection_gradient[picked].astype(jnp.bfloat16)
    hid_back = jnp.dot(mb_grad, head_out.T, preferred_element_type=jnp.float32)
    hid_grad = jnp.where(head_pre > 0, hid_back, 0.0).astype(jnp.bfloat16)
    pool_grad = jnp.dot(hid_grad, head_in.T, preferred_element_type=jnp.float32)
    top_grad = jnp.where(final_pre > 0, (LOSS_SCALE / VOX) * pool_grad[:, None, None, None, :], 0.0)
    inverse = 1.0 / (MICRO * N_DP)

    def one_section(packed):
        section_id, arrived, pre_zero, pre_one, pre_two, reduce_w, spatial_w, expand_w, gain_a, gain_b, gain_c = packed
        out_grad = jnp.where(section_id == SECTIONS - 1, top_grad, arrived.astype(jnp.float32))
        input_grad, grad_reduce, grad_spatial, grad_expand = block_backward(out_grad, pre_zero, pre_one, pre_two, reduce_w, spatial_w, expand_w, gain_a, gain_b, gain_c, inverse)
        return input_grad, grad_reduce.astype(jnp.bfloat16), grad_spatial.astype(jnp.bfloat16), grad_expand.astype(jnp.bfloat16)

    section_ids = jnp.arange(SECTIONS, dtype=jnp.int32)
    input_grad, grad_reduce, grad_spatial, grad_expand = lax.map(one_section, (section_ids, incoming, input_pre, mid_pre1, mid_pre2, w_reduce, w_spatial, w_expand, gain1, gain2, gain3))
    return (projection_gradient, input_grad, grad_reduce, grad_spatial, grad_expand)
```

```python
import jax
import jax.numpy as jnp
from jax import lax
from jax.sharding import Mesh
from jax.sharding import PartitionSpec as P

MICRO = 2


SOFTMAX_TEMP = 0.5
LOSS_SCALE = 1024.0


def shifted(volume, off_a, off_b, off_c):
    extent = volume.shape[1]
    padded = jnp.pad(volume, ((0, 0), (1, 1), (1, 1), (1, 1), (0, 0)))
    return padded[
        :,
        1 + off_a : 1 + off_a + extent,
        1 + off_b : 1 + off_b + extent,
        1 + off_c : 1 + off_c + extent,
        :,
    ]


def block_backward(
    out_grad,
    input_pre,
    mid_pre1,
    mid_pre2,
    w_reduce,
    w_spatial,
    w_expand,
    gain1,
    gain2,
    gain3,
    inverse,
):
    narrow = mid_pre1.shape[-1]
    wide = out_grad.shape[-1]
    e_three = (gain3 * out_grad).astype(jnp.bfloat16)
    flat_three = e_three.reshape(-1, wide)
    hidden_two = jnp.maximum(mid_pre2, 0)
    grad_expand = (
        jnp.dot(hidden_two.reshape(-1, narrow).T, flat_three, preferred_element_type=jnp.float32)
        * inverse
    )
    back_two = jnp.dot(flat_three, w_expand.T, preferred_element_type=jnp.float32).reshape(
        mid_pre2.shape
    )
    e_two = jnp.where(mid_pre2 > 0, gain2 * back_two, 0.0).astype(jnp.bfloat16)
    flat_two = e_two.reshape(-1, narrow)
    hidden_one = jnp.maximum(mid_pre1, 0)
    spatial_parts = []
    back_one = jnp.zeros(mid_pre1.shape, jnp.float32)
    for off_a in (-1, 0, 1):
        block_start = (off_a + 1) * 9 * narrow
        columns = jnp.concatenate(
            [
                shifted(hidden_one, off_a, off_b, off_c)
                for off_b in (-1, 0, 1)
                for off_c in (-1, 0, 1)
            ],
            axis=-1,
        )
        columns = columns.reshape(-1, 9 * narrow)
        spatial_parts.append(
            jnp.dot(columns.T, flat_two, preferred_element_type=jnp.float32) * inverse
        )
        spread = jnp.dot(
            flat_two,
            w_spatial[block_start : block_start + 9 * narrow].T,
            preferred_element_type=jnp.float32,
        )
        spread = spread.reshape(mid_pre1.shape[:-1] + (9, narrow))
        for off_b in (-1, 0, 1):
            for off_c in (-1, 0, 1):
                position = 3 * (off_b + 1) + (off_c + 1)
                back_one = back_one + shifted(spread[..., position, :], -off_a, -off_b, -off_c)
    grad_spatial = jnp.concatenate(spatial_parts, axis=0)
    e_one = jnp.where(mid_pre1 > 0, gain1 * back_one, 0.0).astype(jnp.bfloat16)
    flat_one = e_one.reshape(-1, narrow)
    inputs = jnp.maximum(input_pre, 0)
    grad_reduce = (
        jnp.dot(inputs.reshape(-1, wide).T, flat_one, preferred_element_type=jnp.float32) * inverse
    )
    through = jnp.dot(flat_one, w_reduce.T, preferred_element_type=jnp.float32).reshape(
        out_grad.shape
    )
    input_grad = jnp.where(input_pre > 0, through + out_grad, 0.0).astype(jnp.bfloat16)
    return (input_grad, grad_reduce, grad_spatial, grad_expand)


PLANE = ("x", "y", "core")
DP = ("z_hi", "x", "y", "core")


def copied_to_all(shard, axes, count):
    rows, width = shard.shape
    sent = jnp.broadcast_to(shard[None], (count, rows, width)).reshape(count * rows, width)
    return lax.all_to_all(sent, axes, 0, 0, tiled=True)


def shards(
    projections,
    partner,
    plan,
    head_pre,
    head_in,
    head_out,
    final_pre,
    incoming,
    input_pre,
    mid_pre1,
    mid_pre2,
    w_reduce,
    w_spatial,
    w_expand,
    gain1,
    gain2,
    gain3,
):
    row_peak = lax.Precision.HIGHEST
    row_count, width = projections.shape
    sections = lax.axis_size("section")
    peers = lax.axis_size(PLANE)
    upper = lax.axis_index("z_hi")
    me = lax.axis_index(PLANE)
    swap_near = [
        (half * sections + s, (1 - half) * sections + (s + sections // 2) % sections)
        for half in range(2)
        for s in range(sections)
    ]
    swap_far = [(0, 1), (1, 0)]

    other_rows = lax.ppermute(projections, ("z_hi", "section"), swap_near)
    all_rows = copied_to_all(jnp.concatenate([projections, other_rows], axis=0), PLANE, peers)
    all_crop_rows = all_rows
    first_row = me * 2 * row_count

    half_crops = peers * row_count
    partner_row = (
        (partner % half_crops) // row_count * (2 * row_count)
        + jnp.where(partner // half_crops == upper, 0, row_count)
        + partner % row_count
    )

    scores = jnp.dot(all_crop_rows, all_crop_rows.T, precision=row_peak) / SOFTMAX_TEMP
    column_ids = lax.broadcasted_iota(jnp.int32, scores.shape, 1)
    row_ids = lax.broadcasted_iota(jnp.int32, scores.shape, 0)
    masked = jnp.where(column_ids == row_ids, -jnp.inf, scores)
    largest = jnp.max(masked, axis=0, keepdims=True)
    totals = largest + jnp.log(jnp.sum(jnp.exp(masked - largest), axis=0, keepdims=True))
    mine = lax.dynamic_slice_in_dim(masked, first_row, row_count, 0)
    mine_totals = lax.dynamic_slice_in_dim(totals, first_row, row_count, 1)
    blended = jnp.exp(mine - mine_totals.T) + jnp.exp(mine - totals)
    projection_gradient = (
        jnp.dot(blended, all_crop_rows, precision=row_peak) - 2.0 * all_crop_rows[partner_row]
    ) / SOFTMAX_TEMP
    picked = plan[0, :MICRO]
    mb_grad = projection_gradient[picked].astype(jnp.bfloat16)
    hid_back = jnp.dot(mb_grad, head_out.T, preferred_element_type=jnp.float32)
    hid_grad = jnp.where(head_pre > 0, hid_back, 0.0).astype(jnp.bfloat16)
    pool_part = jnp.dot(hid_grad, head_in.T, preferred_element_type=jnp.float32)
    pool_parts = copied_to_all(pool_part.reshape(-1, width), "section", sections)
    pool_grad = pool_parts.reshape((sections,) + pool_part.shape).sum(axis=0)
    voxels = final_pre.shape[1] * final_pre.shape[2] * final_pre.shape[3]
    top_grad = jnp.where(
        final_pre > 0, LOSS_SCALE / voxels * pool_grad[:, None, None, None, :], 0.0
    )
    is_last = lax.axis_index("section") == sections - 1
    out_grad = jnp.where(is_last, top_grad, incoming[0].astype(jnp.float32))

    narrow = w_reduce.shape[2]
    wide = w_expand.shape[2]
    n_reduce, n_spatial = w_reduce.shape[1], w_spatial.shape[1]
    n_expand = w_expand.shape[1] * wide // narrow
    packed = jnp.concatenate([w_reduce[0], w_spatial[0], w_expand[0].reshape(n_expand, narrow)], axis=0)
    far = lax.ppermute(packed, "z_hi", swap_far)
    ordered = jnp.where(
        upper == 0,
        jnp.concatenate([packed, far], axis=0),
        jnp.concatenate([far, packed], axis=0),
    )
    gathered = copied_to_all(ordered, PLANE, peers).reshape(peers, 2, -1, narrow).swapaxes(0, 1)
    full_reduce = gathered[:, :, :n_reduce].reshape(-1, narrow)
    full_spatial = gathered[:, :, n_reduce : n_reduce + n_spatial].reshape(-1, narrow)
    full_expand = gathered[:, :, n_reduce + n_spatial :].reshape(-1, wide)
    inverse = 1.0 / (MICRO * lax.axis_size(DP))
    input_grad, grad_reduce, grad_spatial, grad_expand = block_backward(
        out_grad,
        input_pre[0],
        mid_pre1[0],
        mid_pre2[0],
        full_reduce,
        full_spatial,
        full_expand,
        gain1[0],
        gain2[0],
        gain3[0],
        inverse,
    )
    devices = 2 * peers
    grads = jnp.concatenate(
        [
            grad_reduce.reshape(devices, n_reduce, narrow),
            grad_spatial.reshape(devices, n_spatial, narrow),
            grad_expand.reshape(devices, n_expand, narrow),
        ],
        axis=1,
    ).astype(jnp.bfloat16)
    rows = grads.shape[1]
    grads = grads.reshape(2, peers, rows, narrow).swapaxes(0, 1).reshape(-1, narrow)
    shares = lax.all_to_all(grads, PLANE, 0, 0, tiled=True).reshape(peers, 2, rows, narrow)
    summed = shares.astype(jnp.float32).sum(axis=0)
    kept = jnp.where(upper == 0, summed[0], summed[1])
    given = jnp.where(upper == 0, summed[1], summed[0])
    total = (kept + lax.ppermute(given, "z_hi", swap_far)).astype(jnp.bfloat16)
    return (
        projection_gradient,
        input_grad[None],
        total[None, :n_reduce],
        total[None, n_reduce : n_reduce + n_spatial],
        total[None, n_reduce + n_spatial :].reshape(w_expand.shape),
    )


def solution(mesh):
    fine = Mesh(
        mesh.devices.reshape(2, 4, 4, 2, mesh.shape["section"]),
        ("z_hi", "x", "y", "core", "section"),
    )
    placed = (
        P(DP, None),
        P(DP),
        P(DP, None),
        P(DP, "section"),
        P(None, "section"),
        P("section", None),
        P(DP, None, None, None, None),
        P("section", DP, None, None, None, None),
        P("section", DP, None, None, None, None),
        P("section", DP, None, None, None, None),
        P("section", DP, None, None, None, None),
        P("section", DP, None),
        P("section", DP, None),
        P("section", DP, None),
        P("section", None),
        P("section", None),
        P("section", None),
    )
    return jax.shard_map(
        shards,
        mesh=fine,
        in_specs=placed,
        out_specs=(
            P(DP, None),
            P("section", DP, None, None, None, None),
            P("section", DP, None),
            P("section", DP, None),
            P("section", DP, None),
        ),
        check_vma=False,
    )
```

```python
import functools

import jax
import jax.numpy as jnp
from jax import lax
from jax.experimental import pallas as pl
from jax.experimental.pallas import tpu as pltpu
from jax.sharding import Mesh
from jax.sharding import PartitionSpec as P

MICRO = 2
SOFTMAX_TEMP = 0.5
LOSS_SCALE = 1024.0
PLANE = ("x", "y", "core")
DP = ("z_hi", "x", "y", "core")
LANES = 128
TILE = 256
BF = jnp.bfloat16
F32 = jnp.float32
ROWS_BY_ROWS = (((1,), (1,)), ((), ()))
VMEM_LIMIT = 20 * 1024 * 1024


def three_parts(values):
    high = values.astype(BF)
    rest = values - high.astype(F32)
    middle = rest.astype(BF)
    return high, middle, (rest - middle.astype(F32)).astype(BF)


def prepare_kernel(
    last_ref, final_ref, incoming_ref, mid1_ref, mid2_ref, input_ref, one_ref, two_ref, in_ref, base_ref
):
    rows, narrow = mid1_ref.shape
    wide = input_ref.shape[1]
    crop_rows = rows // MICRO
    empty = jnp.zeros((64, narrow), BF)
    for crop in range(MICRO):
        at = slice(crop * crop_rows, (crop + 1) * crop_rows)
        hidden = jnp.maximum(mid1_ref[at, :], 0)
        moved = (
            jnp.concatenate([empty, hidden[:-64]], axis=0),
            hidden,
            jnp.concatenate([hidden[64:], empty], axis=0),
        )
        for off_a in range(3):
            one_ref[off_a * narrow : (off_a + 1) * narrow, at] = moved[off_a].T
        two_ref[:, at] = jnp.maximum(mid2_ref[at, :], 0).T
        for part in range(wide // LANES):
            lanes = slice(part * LANES, (part + 1) * LANES)
            in_ref[lanes, at] = jnp.maximum(input_ref[at, lanes], 0).T

    @pl.when(last_ref[0] != 0)
    def _():
        base_ref[...] = jnp.where(final_ref[...].astype(F32) > 0, 1.0, 0.0).astype(BF)

    @pl.when(last_ref[0] == 0)
    def _():
        base_ref[...] = incoming_ref[...]


def prepare_step(last, final, incoming, mid1, mid2, input_pre):
    rows, narrow = mid1.shape
    wide = input_pre.shape[1]
    smem = pl.BlockSpec(memory_space=pltpu.SMEM)
    vmem = pl.BlockSpec(memory_space=pltpu.VMEM)
    return pl.pallas_call(
        prepare_kernel,
        out_shape=(
            jax.ShapeDtypeStruct((3 * narrow, rows), BF),
            jax.ShapeDtypeStruct((narrow, rows), BF),
            jax.ShapeDtypeStruct((wide, rows), BF),
            jax.ShapeDtypeStruct((rows, wide), BF),
        ),
        in_specs=[smem] + [vmem] * 5,
        out_specs=(vmem,) * 4,
        compiler_params=pltpu.CompilerParams(vmem_limit_bytes=VMEM_LIMIT),
        cost_estimate=pl.CostEstimate(flops=0, bytes_accessed=8_000_000, transcendentals=0),
        name="prepare",
    )(last, final, incoming, mid1, mid2, input_pre)


def loss_kernel(
    where_ref,
    plan_ref,
    near_ref,
    across_ref,
    partner_ref,
    head_pre_ref,
    head_in_ref,
    head_out_ref,
    grad_ref,
    pool_ref,
    left,
    right,
    even,
    odd,
    totals,
):
    crops = left.shape[0]
    own = grad_ref.shape[0]
    tiles = crops // TILE
    first = pl.multiple_of(where_ref[0], own)

    for half, rows_ref in enumerate((near_ref, across_ref)):
        count = rows_ref.shape[0]

        def split(r, _, half=half, rows_ref=rows_ref, count=count):
            a, b, c = three_parts(rows_ref[pl.ds(pl.multiple_of(r * TILE, TILE), TILE), :])
            at = pl.ds(pl.multiple_of(half * count + r * TILE, TILE), TILE)
            a2, b2, c2 = a * 2, b * 2, c * 2
            for place, part in enumerate((a2, b2, a2, b2, a2, c2)):
                left[at, place * LANES : (place + 1) * LANES] = part
            for place, part in enumerate((a, a, b, b, c, a)):
                right[at, place * LANES : (place + 1) * LANES] = part
            return 0

        lax.fori_loop(0, count // TILE, split, 0)

    diagonal = lax.broadcasted_iota(jnp.int32, (TILE, TILE), 0) == lax.broadcasted_iota(
        jnp.int32, (TILE, TILE), 1
    )
    groups = crops // 8

    def score_block(j, scores):
        at = pl.ds(pl.multiple_of(j * TILE, TILE), TILE)
        scores[...] = lax.dot_general(
            left[...], right[at, :], ROWS_BY_ROWS, preferred_element_type=F32
        )
        scores[at, :] = jnp.where(diagonal, -jnp.inf, scores[at, :])
        largest = jnp.max(scores[...].reshape(groups, 8, TILE), axis=0)
        return jnp.broadcast_to(jnp.max(largest, axis=0, keepdims=True), (8, TILE))

    def sum_block(j, scores, largest):
        at = pl.ds(pl.multiple_of(j * TILE, TILE), TILE)
        summed = jnp.sum(jnp.exp(scores[...].reshape(groups, 8, TILE) - largest[None]), axis=0)
        whole = jnp.broadcast_to(jnp.sum(summed, axis=0, keepdims=True), (8, TILE))
        totals[:, at] = largest + jnp.log(whole)

    def two_blocks(pair, largest):
        j = 2 * pair
        following = score_block(j + 1, odd)
        sum_block(j, even, largest)
        after = score_block(j + 2, even)
        sum_block(j + 1, odd, following)
        return after

    largest = lax.fori_loop(0, tiles // 2 - 1, two_blocks, score_block(0, even))
    following = score_block(tiles - 1, odd)
    sum_block(tiles - 2, even, largest)
    sum_block(tiles - 1, odd, following)

    mine = lax.dot_general(
        left[pl.ds(first, own), :], right[...], ROWS_BY_ROWS, preferred_element_type=F32
    )
    columns = lax.broadcasted_iota(jnp.int32, (own, crops), 1)
    mine = jnp.where(
        columns == lax.broadcasted_iota(jnp.int32, (own, crops), 0) + first, -jnp.inf, mine
    )
    peak = jnp.max(mine, axis=1, keepdims=True)
    my_totals = peak + jnp.log(jnp.sum(jnp.exp(mine - peak), axis=1, keepdims=True))
    blended = jnp.exp(mine - my_totals) + jnp.exp(mine - totals[0:1, :])
    blended = blended - jnp.where(columns == partner_ref[...], 2.0, 0.0)
    a, b, c = three_parts(blended)
    stacked = jnp.concatenate([a, b, c], axis=0)
    products = jnp.dot(stacked, right[:, LANES : 3 * LANES], preferred_element_type=F32)
    low = jnp.dot(a, right[:, 4 * LANES : 5 * LANES], preferred_element_type=F32)
    small = products[own : 2 * own, LANES:] + products[2 * own :, :LANES] + low
    gradient = (
        products[:own, :LANES] + (products[:own, LANES:] + products[own : 2 * own, :LANES] + small)
    ) / SOFTMAX_TEMP
    grad_ref[...] = gradient

    pick_row = lax.broadcasted_iota(jnp.int32, (16, own), 0)
    pick_column = lax.broadcasted_iota(jnp.int32, (16, own), 1)
    wanted = jnp.where(pick_row == 0, plan_ref[0, 0], plan_ref[0, 1])
    chosen = jnp.where((pick_column == wanted) & (pick_row < MICRO), 1.0, 0.0).astype(BF)
    picked = jnp.dot(chosen, gradient.astype(BF), preferred_element_type=F32).astype(BF)
    hid_back = lax.dot_general(
        picked, head_out_ref[...], ROWS_BY_ROWS, preferred_element_type=F32
    )
    hid_grad = jnp.where(head_pre_ref[...].astype(F32) > 0, hid_back[:MICRO], 0.0)
    hid_grad = jnp.concatenate(
        [hid_grad, jnp.zeros((16 - MICRO, hid_grad.shape[1]), F32)], axis=0
    ).astype(BF)
    pool = lax.dot_general(hid_grad, head_in_ref[...], ROWS_BY_ROWS, preferred_element_type=F32)
    parts = pool.shape[1] // LANES
    packed = jnp.concatenate(
        [pool[m : m + 1, n * LANES : (n + 1) * LANES] for m in range(MICRO) for n in range(parts)],
        axis=0,
    )
    for copy in range(pool_ref.shape[0] // packed.shape[0]):
        pool_ref[copy * packed.shape[0] : (copy + 1) * packed.shape[0], :] = packed


def loss_step(first_row, plan, near, across, partner_row, head_pre, head_in, head_out, own, sections):
    crops, width = 2 * near.shape[0], near.shape[1]
    pool_rows = MICRO * head_in.shape[0] // LANES
    smem = pl.BlockSpec(memory_space=pltpu.SMEM)
    vmem = pl.BlockSpec(memory_space=pltpu.VMEM)
    return pl.pallas_call(
        loss_kernel,
        out_shape=(
            jax.ShapeDtypeStruct((own, width), F32),
            jax.ShapeDtypeStruct((sections * pool_rows, LANES), F32),
        ),
        in_specs=[smem, smem] + [vmem] * 6,
        out_specs=(vmem, vmem),
        scratch_shapes=[
            pltpu.VMEM((crops, 6 * LANES), BF),
            pltpu.VMEM((crops, 6 * LANES), BF),
            pltpu.VMEM((crops, TILE), F32),
            pltpu.VMEM((crops, TILE), F32),
            pltpu.VMEM((8, crops), F32),
        ],
        compiler_params=pltpu.CompilerParams(vmem_limit_bytes=VMEM_LIMIT),
        cost_estimate=pl.CostEstimate(
            flops=12_000_000_000, bytes_accessed=2_000_000, transcendentals=4_000_000
        ),
        name="loss",
    )(first_row, plan, near, across, partner_row, head_pre, head_in, head_out)


def pooled_scale(last, pool_ref, voxels):
    rows = MICRO * 4
    total = pool_ref[0:rows, :]
    for source in range(1, pool_ref.shape[0] // rows):
        total = total + pool_ref[source * rows : (source + 1) * rows, :]
    return jnp.where(last, total * (LOSS_SCALE / voxels), 1.0)


def out_grad_tile(scale, crop, part, base):
    return base.astype(F32) * scale[crop * 4 + part : crop * 4 + part + 1, :]


def block_kernel(
    where_ref,
    pool_ref,
    base_ref,
    mid1_ref,
    mid2_ref,
    turned1_ref,
    turned2_ref,
    turned_in_ref,
    spatial_ref,
    expand_ref,
    gain1_ref,
    gain2_ref,
    gain3_ref,
    kept_ref,
    given_ref,
    e_one_ref,
    e_three,
    shifts,
    spatial_sum,
    expand_sum,
    reduce_sum,
    chunk,
):
    side = 8
    rows, narrow = mid1_ref.shape
    wide = e_three.shape[1]
    crop_rows = rows // MICRO
    plane = side * side
    inverse = 1.0 / (MICRO * 64)
    scale = pooled_scale(where_ref[0] != 0, pool_ref, side * plane)

    step = 256
    for start in range(0, rows, step):
        crop = start // crop_rows
        for part in range(wide // LANES):
            lanes = slice(part * LANES, (part + 1) * LANES)
            at = slice(start, start + step)
            out_grad = out_grad_tile(scale, crop, part, base_ref[at, lanes])
            e_three[at, lanes] = (gain3_ref[:, lanes] * out_grad).astype(BF)

    expand_sum[...] = jnp.dot(turned2_ref[...], e_three[...], preferred_element_type=F32) * inverse

    for start in range(0, rows, crop_rows):
        at = slice(start, start + crop_rows)
        back = lax.dot_general(
            e_three[at, :], expand_ref[...], ROWS_BY_ROWS, preferred_element_type=F32
        )
        e_two = jnp.where(mid2_ref[at, :].astype(F32) > 0, gain2_ref[...] * back, 0.0)
        e_two = e_two.astype(BF).astype(F32).reshape(plane, side, narrow)
        place = lax.broadcasted_iota(jnp.int32, e_two.shape, 1)
        none = jnp.zeros((side, 1, side, narrow), F32)
        for off_c in (-1, 0, 1):
            if off_c == 0:
                moved = e_two
            elif off_c == 1:
                moved = jnp.where(place == 0, 0.0, pltpu.roll(e_two, 1, 1))
            else:
                moved = jnp.where(place == side - 1, 0.0, pltpu.roll(e_two, side - 1, 1))
            moved = moved.reshape(side, side, side, narrow)
            for off_b in (-1, 0, 1):
                if off_b == 0:
                    both = moved
                elif off_b == 1:
                    both = jnp.concatenate([none, moved[:, :-1]], axis=1)
                else:
                    both = jnp.concatenate([moved[:, 1:], none], axis=1)
                position = 3 * (off_b + 1) + (off_c + 1)
                shifts[at, position * narrow : (position + 1) * narrow] = both.reshape(
                    crop_rows, narrow
                ).astype(BF)

    empty = jnp.zeros((plane, narrow), F32)
    for crop in range(MICRO):
        at = slice(crop * crop_rows, (crop + 1) * crop_rows)
        spread = lax.dot_general(
            shifts[at, :], spatial_ref[...], ROWS_BY_ROWS, preferred_element_type=F32
        )
        lower = jnp.concatenate([spread[plane:, :narrow], empty], axis=0)
        upper = jnp.concatenate([empty, spread[:-plane, 2 * narrow :]], axis=0)
        back_one = lower + spread[:, narrow : 2 * narrow] + upper
        e_one_ref[at, :] = jnp.where(
            mid1_ref[at, :].astype(F32) > 0, gain1_ref[...] * back_one, 0.0
        ).astype(BF)

    reduce_sum[...] = (
        jnp.dot(turned_in_ref[...], e_one_ref[...], preferred_element_type=F32) * inverse
    )

    for off_a in range(3):
        summed = (
            jnp.dot(
                turned1_ref[off_a * narrow : (off_a + 1) * narrow, :],
                shifts[...],
                preferred_element_type=F32,
            )
            * inverse
        )
        for position in range(9):
            block = off_a * 9 + position
            spatial_sum[block * narrow : (block + 1) * narrow, :] = summed[
                :, position * narrow : (position + 1) * narrow
            ]

    chips = 16
    height = kept_ref.shape[0] // chips
    chunk[140:144, :] = jnp.zeros((4, narrow), F32)

    def pack(chip, to, out_ref):
        for half in range(2):
            device = half * 2 * chips + chip * 2 + to
            chunk[half * 8 : half * 8 + 8, :] = reduce_sum[device * 8 : device * 8 + 8, :]
            for part in range(4):
                chunk[16 + half * 8 + part * 2 : 18 + half * 8 + part * 2, :] = expand_sum[
                    device * 2 : device * 2 + 2, part * LANES : (part + 1) * LANES
                ]
            chunk[32 + half * 54 : 86 + half * 54, :] = spatial_sum[
                device * 54 : device * 54 + 54, :
            ]
        out_ref[chip * height : (chip + 1) * height, :] = chunk[...].astype(BF)

    for core in range(2):

        @pl.when(where_ref[1] == core)
        def _(core=core):
            for chip in range(chips):
                pack(chip, core, kept_ref)
                pack(chip, 1 - core, given_ref)


def block_step(place, pool, base, mid1, mid2, turned1, turned2, turned_in, spatial, expand, gains):
    rows, narrow = mid1.shape
    wide = base.shape[1]
    smem = pl.BlockSpec(memory_space=pltpu.SMEM)
    vmem = pl.BlockSpec(memory_space=pltpu.VMEM)
    return pl.pallas_call(
        block_kernel,
        out_shape=(
            jax.ShapeDtypeStruct((16 * 144, narrow), BF),
            jax.ShapeDtypeStruct((16 * 144, narrow), BF),
            jax.ShapeDtypeStruct((rows, narrow), BF),
        ),
        in_specs=[smem] + [vmem] * 12,
        out_specs=(vmem, vmem, vmem),
        scratch_shapes=[
            pltpu.VMEM((rows, wide), BF),
            pltpu.VMEM((rows, 9 * narrow), BF),
            pltpu.VMEM((27 * narrow, narrow), F32),
            pltpu.VMEM((narrow, wide), F32),
            pltpu.VMEM((wide, narrow), F32),
            pltpu.VMEM((144, narrow), F32),
        ],
        compiler_params=pltpu.CompilerParams(vmem_limit_bytes=VMEM_LIMIT),
        cost_estimate=pl.CostEstimate(
            flops=4_000_000_000, bytes_accessed=6_000_000, transcendentals=0
        ),
        name="block",
    )(place, pool, base, mid1, mid2, turned1, turned2, turned_in, spatial, expand, *gains)


def input_kernel(where_ref, pool_ref, base_ref, input_ref, e_one_ref, reduce_ref, out_ref):
    rows, wide = input_ref.shape
    crop_rows = rows // MICRO
    scale = pooled_scale(where_ref[0] != 0, pool_ref, crop_rows)
    step = 256
    for start in range(0, rows, step):
        at = slice(start, start + step)
        through = lax.dot_general(
            e_one_ref[at, :], reduce_ref[...], ROWS_BY_ROWS, preferred_element_type=F32
        )
        for part in range(wide // LANES):
            lanes = slice(part * LANES, (part + 1) * LANES)
            out_grad = out_grad_tile(scale, start // crop_rows, part, base_ref[at, lanes])
            out_ref[at, lanes] = jnp.where(
                input_ref[at, lanes].astype(F32) > 0, through[:, lanes] + out_grad, 0.0
            ).astype(BF)


def input_step(place, pool, base, input_pre, e_one, reduce):
    smem = pl.BlockSpec(memory_space=pltpu.SMEM)
    vmem = pl.BlockSpec(memory_space=pltpu.VMEM)
    return pl.pallas_call(
        input_kernel,
        out_shape=jax.ShapeDtypeStruct(input_pre.shape, BF),
        in_specs=[smem] + [vmem] * 5,
        out_specs=vmem,
        compiler_params=pltpu.CompilerParams(vmem_limit_bytes=VMEM_LIMIT),
        cost_estimate=pl.CostEstimate(
            flops=200_000_000, bytes_accessed=6_000_000, transcendentals=0
        ),
        name="input_grad",
    )(place, pool, base, input_pre, e_one, reduce)


def sum_kernel(half_ref, shares_ref, kept_ref, given_ref, total):
    height = total.shape[0]
    summed = shares_ref[0:height, :].astype(F32)
    for source in range(1, shares_ref.shape[0] // height):
        summed = summed + shares_ref[source * height : (source + 1) * height, :].astype(F32)
    total[...] = summed

    def put(target, half):
        target[0:8, :] = total[half * 8 : half * 8 + 8, :]
        target[8:16, :] = total[16 + half * 8 : 24 + half * 8, :]
        target[16:72, :] = total[32 + half * 54 : 88 + half * 54, :]

    @pl.when(half_ref[0] == 0)
    def _():
        put(kept_ref, 0)
        put(given_ref, 1)

    @pl.when(half_ref[0] != 0)
    def _():
        put(kept_ref, 1)
        put(given_ref, 0)


def sum_step(half, shares):
    smem = pl.BlockSpec(memory_space=pltpu.SMEM)
    vmem = pl.BlockSpec(memory_space=pltpu.VMEM)
    shape = jax.ShapeDtypeStruct((72, LANES), F32)
    return pl.pallas_call(
        sum_kernel,
        out_shape=(shape, shape),
        in_specs=[smem, vmem],
        out_specs=(vmem, vmem),
        scratch_shapes=[pltpu.VMEM((144, LANES), F32)],
        compiler_params=pltpu.CompilerParams(vmem_limit_bytes=VMEM_LIMIT),
        name="shares",
    )(half, shares)


def last_kernel(kept_ref, got_ref, reduce_ref, spatial_ref, expand_ref):
    total = kept_ref[...] + got_ref[...]
    reduce_ref[...] = total[0:8, :].astype(BF)
    spatial_ref[...] = total[16:70, :].astype(BF)
    expand_ref[...] = jnp.concatenate(
        [total[8 + 2 * part : 10 + 2 * part, :] for part in range(4)], axis=1
    ).astype(BF)


def last_step(kept, got):
    vmem = pl.BlockSpec(memory_space=pltpu.VMEM)
    return pl.pallas_call(
        last_kernel,
        out_shape=(
            jax.ShapeDtypeStruct((8, LANES), BF),
            jax.ShapeDtypeStruct((54, LANES), BF),
            jax.ShapeDtypeStruct((2, 4 * LANES), BF),
        ),
        in_specs=[vmem] * 2,
        out_specs=(vmem,) * 3,
        name="weight_grads",
    )(kept, got)


def copies(shard, count):
    rows, width = shard.shape
    return jnp.broadcast_to(shard[None], (count, rows, width)).reshape(count * rows, width)


def shards(
    projections,
    partner,
    plan,
    head_pre,
    head_in,
    head_out,
    final_pre,
    incoming,
    input_pre,
    mid_pre1,
    mid_pre2,
    w_reduce,
    w_spatial,
    w_expand,
    gain1,
    gain2,
    gain3,
):
    row_count = projections.shape[0]
    sections = lax.axis_size("section")
    peers = lax.axis_size(PLANE)
    upper = lax.axis_index("z_hi")
    me = lax.axis_index(PLANE)
    swap_near = [
        (half * sections + s, (1 - half) * sections + (s + sections // 2) % sections)
        for half in range(2)
        for s in range(sections)
    ]
    swap_far = [(0, 1), (1, 0)]
    narrow = w_reduce.shape[2]
    wide = w_expand.shape[2]
    core = lax.axis_index("core")
    section = lax.axis_index("section")
    chips = peers // 2
    other_rows = lax.ppermute(projections, ("z_hi", "section"), swap_near)
    n_reduce, n_spatial = w_reduce.shape[1], w_spatial.shape[1]
    n_expand = w_expand.shape[1] * wide // narrow
    packed = jnp.concatenate(
        [w_reduce[0], w_spatial[0], w_expand[0].reshape(n_expand, narrow)], axis=0
    )
    flat_one = mid_pre1.reshape(-1, narrow)
    flat_two = mid_pre2.reshape(-1, narrow)
    flat_in = input_pre.reshape(-1, wide)
    flat_final = final_pre.reshape(-1, wide)
    flat_incoming = incoming.reshape(-1, wide)
    is_last = section == sections - 1
    place = jnp.stack([is_last.astype(jnp.int32), core.astype(jnp.int32)])
    sent, packed, saved_one, saved_two = lax.optimization_barrier(
        (
            copies(jnp.concatenate([projections, other_rows], axis=0), chips),
            packed,
            flat_one,
            flat_two,
        )
    )
    near = lax.all_to_all(sent, ("x", "y"), 0, 0, tiled=True)
    far = lax.ppermute(packed, "z_hi", swap_far)
    turned_one, turned_two, turned_in, base = prepare_step(
        place, flat_final, flat_incoming, saved_one, saved_two, flat_in
    )
    ordered = jnp.where(
        upper == 0,
        jnp.concatenate([packed, far], axis=0),
        jnp.concatenate([far, packed], axis=0),
    )
    near, weights, turned_one, turned_two, turned_in, base = lax.optimization_barrier(
        (near, copies(ordered, peers), turned_one, turned_two, turned_in, base)
    )
    across = lax.ppermute(near, "core", swap_far)
    half_crops = peers * row_count
    partner_device = partner % half_crops // row_count
    partner_row = (
        jnp.where(partner_device % 2 == core, 0, half_crops)
        + partner_device // 2 * (2 * row_count)
        + jnp.where(partner // half_crops == upper, 0, row_count)
        + partner % row_count
    )

    gathered = lax.all_to_all(weights, PLANE, 0, 0, tiled=True)
    gathered = gathered.reshape(peers, 2, -1, narrow).swapaxes(0, 1)
    full_reduce = gathered[:, :, :n_reduce].reshape(-1, narrow)
    full_spatial = (
        gathered[:, :, n_reduce : n_reduce + n_spatial]
        .reshape(3, 9, narrow, narrow)
        .swapaxes(1, 2)
        .reshape(3 * narrow, 9 * narrow)
    )
    full_expand = gathered[:, :, n_reduce + n_spatial :].reshape(-1, wide)

    projection_gradient, pool_copies = loss_step(
        (me // 2 * 2 * row_count).reshape(1),
        plan,
        near,
        across,
        partner_row.reshape(-1, 1),
        head_pre,
        head_in,
        head_out,
        row_count,
        sections,
    )
    pool = lax.all_to_all(pool_copies, "section", 0, 0, tiled=True)
    kept, given, e_one = block_step(
        place,
        pool,
        base,
        flat_one,
        flat_two,
        turned_one,
        turned_two,
        turned_in,
        full_spatial,
        full_expand,
        (gain1, gain2, gain3),
    )
    got = lax.ppermute(given, "core", swap_far)
    paired = (kept.astype(F32) + got.astype(F32)).astype(BF)
    shares = lax.all_to_all(paired, ("x", "y"), 0, 0, tiled=True)
    input_grad = input_step(place, pool, base, flat_in, e_one, full_reduce)
    kept, given = sum_step(upper.astype(jnp.int32).reshape(1), shares)
    got = lax.ppermute(given, "z_hi", swap_far)
    sum_reduce, sum_spatial, sum_expand = last_step(kept, got)
    return (
        projection_gradient,
        input_grad.reshape(input_pre.shape),
        sum_reduce[None],
        sum_spatial[None],
        sum_expand[None],
    )


def solution(mesh):
    fine = Mesh(
        mesh.devices.reshape(2, 4, 4, 2, mesh.shape["section"]),
        ("z_hi", "x", "y", "core", "section"),
    )
    placed = (
        P(DP, None),
        P(DP),
        P(DP, None),
        P(DP, "section"),
        P(None, "section"),
        P("section", None),
        P(DP, None, None, None, None),
        P("section", DP, None, None, None, None),
        P("section", DP, None, None, None, None),
        P("section", DP, None, None, None, None),
        P("section", DP, None, None, None, None),
        P("section", DP, None),
        P("section", DP, None),
        P("section", DP, None),
        P("section", None),
        P("section", None),
        P("section", None),
    )
    return jax.shard_map(
        shards,
        mesh=fine,
        in_specs=placed,
        out_specs=(
            P(DP, None),
            P("section", DP, None, None, None, None),
            P("section", DP, None),
            P("section", DP, None),
            P("section", DP, None),
        ),
        check_vma=False,
    )
```

```python
import functools

import jax
import jax.numpy as jnp
from jax import lax
from jax.experimental import pallas as pl
from jax.experimental.pallas import tpu as pltpu
from jax.sharding import Mesh
from jax.sharding import PartitionSpec as P

MICRO = 2
SOFTMAX_TEMP = 0.5
LOSS_SCALE = 1024.0
PLANE = ("x", "y", "core")
DP = ("z_hi", "x", "y", "core")
LANES = 128
TILE = 256
BF = jnp.bfloat16
F32 = jnp.float32
ROWS_BY_ROWS = (((1,), (1,)), ((), ()))
VMEM_LIMIT = 24 * 1024 * 1024


def three_parts(values):
    high = values.astype(BF)
    rest = values - high.astype(F32)
    middle = rest.astype(BF)
    return high, middle, (rest - middle.astype(F32)).astype(BF)


def prepare_kernel(
    where_ref,
    near_hbm,
    across_hbm,
    final_hbm,
    incoming_hbm,
    mid1_hbm,
    mid2_hbm,
    input_hbm,
    one_hbm,
    two_hbm,
    in_hbm,
    base_hbm,
    spatial_hbm,
    expand_hbm,
    reduce_hbm,
    near_ref,
    across_ref,
    final_ref,
    mid1_ref,
    mid2_ref,
    input_ref,
    one_ref,
    two_ref,
    in_ref,
    base_ref,
    spatial_ref,
    expand_ref,
    reduce_ref,
    spatial_rows,
    expand_rows,
    reduce_rows,
    read_sems,
    write_sems,
):
    rows, narrow = mid1_ref.shape
    wide = input_ref.shape[1]
    crop_rows = rows // MICRO
    reads = [
        pltpu.make_async_copy(source, target, read_sems.at[place])
        for place, (source, target) in enumerate(
            (
                (mid1_hbm, mid1_ref),
                (mid2_hbm, mid2_ref),
                (input_hbm, input_ref),
                (near_hbm, near_ref),
                (across_hbm, across_ref),
            )
        )
    ]
    writes = [
        pltpu.make_async_copy(source, target, write_sems.at[place])
        for place, (source, target) in enumerate(
            (
                (one_ref, one_hbm),
                (two_ref, two_hbm),
                (in_ref, in_hbm),
                (base_ref, base_hbm),
                (spatial_ref, spatial_hbm),
                (expand_ref, expand_hbm),
                (reduce_ref, reduce_hbm),
            )
        )
    ]
    for read in reads:
        read.start()

    @pl.when(where_ref[0] != 0)
    def _():
        read = pltpu.make_async_copy(final_hbm, final_ref, read_sems.at[5])
        read.start()
        read.wait()
        base_ref[...] = jnp.where(final_ref[...].astype(F32) > 0, 1.0, 0.0).astype(BF)

    @pl.when(where_ref[0] == 0)
    def _():
        read = pltpu.make_async_copy(incoming_hbm, base_ref, read_sems.at[5])
        read.start()
        read.wait()

    writes[3].start()
    empty = jnp.zeros((64, narrow), BF)
    reads[0].wait()
    for crop in range(MICRO):
        at = slice(crop * crop_rows, (crop + 1) * crop_rows)
        hidden = jnp.maximum(mid1_ref[at, :], 0)
        moved = (
            jnp.concatenate([empty, hidden[:-64]], axis=0),
            hidden,
            jnp.concatenate([hidden[64:], empty], axis=0),
        )
        for off_a in range(3):
            one_ref[off_a * narrow : (off_a + 1) * narrow, at] = moved[off_a].T
    writes[0].start()
    reads[1].wait()
    two_ref[...] = jnp.maximum(mid2_ref[...], 0).T
    writes[1].start()
    reads[2].wait()
    for part in range(wide // LANES):
        lanes = slice(part * LANES, (part + 1) * LANES)
        in_ref[lanes, :] = jnp.maximum(input_ref[:, lanes], 0).T
    writes[2].start()
    reads[3].wait()
    reads[4].wait()

    chips = near_ref.shape[0] // 144

    def unpack(source, chip, core):
        shard = source[chip * 144 : (chip + 1) * 144, :].astype(F32)
        for half in range(2):
            device = half * 2 * chips + chip * 2 + core
            top = half * 72
            reduce_rows[device * 8 : device * 8 + 8, :] = shard[top : top + 8]
            for part in range(8):
                row, lane = device * 2 + part // 4, part % 4 * LANES
                expand_rows[row : row + 1, lane : lane + LANES] = shard[
                    top + 8 + part : top + 9 + part
                ]
            spatial_rows[device * 54 : device * 54 + 54, :] = shard[top + 16 : top + 70]

    for core in range(2):

        @pl.when(where_ref[1] == core)
        def _(core=core):
            for chip in range(chips):
                unpack(near_ref, chip, core)
                unpack(across_ref, chip, 1 - core)

    reduce_ref[...] = reduce_rows[...].astype(BF)
    expand_ref[...] = expand_rows[...].astype(BF)
    for off_a in range(3):
        for position in range(9):
            block = off_a * 9 + position
            spatial_ref[
                off_a * narrow : (off_a + 1) * narrow, position * narrow : (position + 1) * narrow
            ] = spatial_rows[block * narrow : (block + 1) * narrow, :].astype(BF)
    for write in writes[4:]:
        write.start()
    for write in writes:
        write.wait()


def prepare_step(place, near, across, final, incoming, mid1, mid2, input_pre):
    rows, narrow = mid1.shape
    wide = input_pre.shape[1]
    smem = pl.BlockSpec(memory_space=pltpu.SMEM)
    hbm = pl.BlockSpec(memory_space=pltpu.HBM)
    outs = (
        (3 * narrow, rows),
        (narrow, rows),
        (wide, rows),
        (rows, wide),
        (3 * narrow, 9 * narrow),
        (narrow, wide),
        (wide, narrow),
    )
    held = [near.shape, across.shape, final.shape, mid1.shape, mid2.shape, input_pre.shape]
    return pl.pallas_call(
        prepare_kernel,
        out_shape=tuple(pltpu.HBM(shape, BF) for shape in outs),
        in_specs=[smem] + [hbm] * 7,
        out_specs=(hbm,) * 7,
        scratch_shapes=[pltpu.VMEM(shape, BF) for shape in (*held, *outs)]
        + [
            pltpu.VMEM((27 * narrow, narrow), F32),
            pltpu.VMEM((narrow, wide), F32),
            pltpu.VMEM((wide, narrow), F32),
            pltpu.SemaphoreType.DMA((6,)),
            pltpu.SemaphoreType.DMA((7,)),
        ],
        compiler_params=pltpu.CompilerParams(vmem_limit_bytes=VMEM_LIMIT),
        cost_estimate=pl.CostEstimate(flops=0, bytes_accessed=9_000_000, transcendentals=0),
        name="prepare",
    )(place, *in_hbm(near, across, final, incoming, mid1, mid2, input_pre))


def loss_kernel(
    where_ref,
    plan_ref,
    near_hbm,
    across_hbm,
    partner_ref,
    head_pre_ref,
    head_in_ref,
    head_out_ref,
    grad_ref,
    pool_ref,
    left,
    right,
    even,
    odd,
    totals,
    near_ref,
    across_ref,
    read_sems,
):
    crops = left.shape[0]
    own = grad_ref.shape[0]
    tiles = crops // TILE
    first = pl.multiple_of(where_ref[0], own)

    reads = [
        pltpu.make_async_copy(near_hbm, near_ref, read_sems.at[0]),
        pltpu.make_async_copy(across_hbm, across_ref, read_sems.at[1]),
    ]
    for read in reads:
        read.start()
    for half, rows_ref in enumerate((near_ref, across_ref)):
        count = rows_ref.shape[0]
        reads[half].wait()

        def split(r, _, half=half, rows_ref=rows_ref, count=count):
            a, b, c = three_parts(rows_ref[pl.ds(pl.multiple_of(r * TILE, TILE), TILE), :])
            at = pl.ds(pl.multiple_of(half * count + r * TILE, TILE), TILE)
            a2, b2, c2 = a * 2, b * 2, c * 2
            for place, part in enumerate((a2, b2, a2, b2, a2, c2)):
                left[at, place * LANES : (place + 1) * LANES] = part
            for place, part in enumerate((a, a, b, b, c, a)):
                right[at, place * LANES : (place + 1) * LANES] = part
            return 0

        lax.fori_loop(0, count // TILE, split, 0)

    diagonal = lax.broadcasted_iota(jnp.int32, (TILE, TILE), 0) == lax.broadcasted_iota(
        jnp.int32, (TILE, TILE), 1
    )
    groups = crops // 8

    def score_block(j, scores):
        at = pl.ds(pl.multiple_of(j * TILE, TILE), TILE)
        scores[...] = lax.dot_general(
            left[...], right[at, :], ROWS_BY_ROWS, preferred_element_type=F32
        )
        scores[at, :] = jnp.where(diagonal, -jnp.inf, scores[at, :])
        largest = jnp.max(scores[...].reshape(groups, 8, TILE), axis=0)
        return jnp.broadcast_to(jnp.max(largest, axis=0, keepdims=True), (8, TILE))

    def sum_block(j, scores, largest):
        at = pl.ds(pl.multiple_of(j * TILE, TILE), TILE)
        summed = jnp.sum(jnp.exp(scores[...].reshape(groups, 8, TILE) - largest[None]), axis=0)
        whole = jnp.broadcast_to(jnp.sum(summed, axis=0, keepdims=True), (8, TILE))
        totals[:, at] = largest + jnp.log(whole)

    def two_blocks(pair, largest):
        j = 2 * pair
        following = score_block(j + 1, odd)
        sum_block(j, even, largest)
        after = score_block(j + 2, even)
        sum_block(j + 1, odd, following)
        return after

    largest = lax.fori_loop(0, tiles // 2 - 1, two_blocks, score_block(0, even))
    following = score_block(tiles - 1, odd)
    sum_block(tiles - 2, even, largest)
    sum_block(tiles - 1, odd, following)

    mine = lax.dot_general(
        left[pl.ds(first, own), :], right[...], ROWS_BY_ROWS, preferred_element_type=F32
    )
    columns = lax.broadcasted_iota(jnp.int32, (own, crops), 1)
    mine = jnp.where(
        columns == lax.broadcasted_iota(jnp.int32, (own, crops), 0) + first, -jnp.inf, mine
    )
    peak = jnp.max(mine, axis=1, keepdims=True)
    my_totals = peak + jnp.log(jnp.sum(jnp.exp(mine - peak), axis=1, keepdims=True))
    blended = jnp.exp(mine - my_totals) + jnp.exp(mine - totals[0:1, :])
    blended = blended - jnp.where(columns == partner_ref[...], 2.0, 0.0)
    a, b, c = three_parts(blended)
    stacked = jnp.concatenate([a, b, c], axis=0)
    products = jnp.dot(stacked, right[:, LANES : 3 * LANES], preferred_element_type=F32)
    low = jnp.dot(a, right[:, 4 * LANES : 5 * LANES], preferred_element_type=F32)
    small = products[own : 2 * own, LANES:] + products[2 * own :, :LANES] + low
    gradient = (
        products[:own, :LANES] + (products[:own, LANES:] + products[own : 2 * own, :LANES] + small)
    ) / SOFTMAX_TEMP
    grad_ref[...] = gradient

    pick_row = lax.broadcasted_iota(jnp.int32, (16, own), 0)
    pick_column = lax.broadcasted_iota(jnp.int32, (16, own), 1)
    wanted = jnp.where(pick_row == 0, plan_ref[0, 0], plan_ref[0, 1])
    chosen = jnp.where((pick_column == wanted) & (pick_row < MICRO), 1.0, 0.0).astype(BF)
    picked = jnp.dot(chosen, gradient.astype(BF), preferred_element_type=F32).astype(BF)
    hid_back = lax.dot_general(
        picked, head_out_ref[...], ROWS_BY_ROWS, preferred_element_type=F32
    )
    hid_grad = jnp.where(head_pre_ref[...].astype(F32) > 0, hid_back[:MICRO], 0.0)
    hid_grad = jnp.concatenate(
        [hid_grad, jnp.zeros((16 - MICRO, hid_grad.shape[1]), F32)], axis=0
    ).astype(BF)
    pool = lax.dot_general(hid_grad, head_in_ref[...], ROWS_BY_ROWS, preferred_element_type=F32)
    parts = pool.shape[1] // LANES
    packed = jnp.concatenate(
        [pool[m : m + 1, n * LANES : (n + 1) * LANES] for m in range(MICRO) for n in range(parts)],
        axis=0,
    )
    for copy in range(pool_ref.shape[0] // packed.shape[0]):
        pool_ref[copy * packed.shape[0] : (copy + 1) * packed.shape[0], :] = packed


def loss_step(first_row, plan, near, across, partner_row, head_pre, head_in, head_out, own, sections):
    crops, width = 2 * near.shape[0], near.shape[1]
    pool_rows = MICRO * head_in.shape[0] // LANES
    smem = pl.BlockSpec(memory_space=pltpu.SMEM)
    vmem = pl.BlockSpec(memory_space=pltpu.VMEM)
    hbm = pl.BlockSpec(memory_space=pltpu.HBM)
    return pl.pallas_call(
        loss_kernel,
        out_shape=(
            jax.ShapeDtypeStruct((own, width), F32),
            jax.ShapeDtypeStruct((sections * pool_rows, LANES), F32),
        ),
        in_specs=[smem, smem, hbm, hbm] + [vmem] * 4,
        out_specs=(vmem, vmem),
        scratch_shapes=[
            pltpu.VMEM((crops, 6 * LANES), BF),
            pltpu.VMEM((crops, 6 * LANES), BF),
            pltpu.VMEM((crops, TILE), F32),
            pltpu.VMEM((crops, TILE), F32),
            pltpu.VMEM((8, crops), F32),
            pltpu.VMEM(near.shape, F32),
            pltpu.VMEM(across.shape, F32),
            pltpu.SemaphoreType.DMA((2,)),
        ],
        compiler_params=pltpu.CompilerParams(vmem_limit_bytes=VMEM_LIMIT),
        cost_estimate=pl.CostEstimate(
            flops=12_000_000_000, bytes_accessed=2_000_000, transcendentals=4_000_000
        ),
        name="loss",
    )(first_row, plan, *in_hbm(near, across), partner_row, head_pre, head_in, head_out)


def pooled_scale(last, pool_ref, voxels):
    rows = MICRO * 4
    total = pool_ref[0:rows, :]
    for source in range(1, pool_ref.shape[0] // rows):
        total = total + pool_ref[source * rows : (source + 1) * rows, :]
    return jnp.where(last, total * (LOSS_SCALE / voxels), 1.0)


def out_grad_tile(scale, crop, part, base):
    return base.astype(F32) * scale[crop * 4 + part : crop * 4 + part + 1, :]


def block_kernel(
    where_ref,
    pool_ref,
    base_hbm,
    mid1_hbm,
    mid2_hbm,
    turned1_hbm,
    turned2_hbm,
    turned_in_hbm,
    spatial_hbm,
    expand_hbm,
    gain1_ref,
    gain2_ref,
    gain3_ref,
    kept_ref,
    given_ref,
    e_one_ref,
    e_three,
    shifts,
    spatial_sum,
    expand_sum,
    reduce_sum,
    chunk,
    base_ref,
    expand_ref,
    mid2_ref,
    turned2_ref,
    spatial_ref,
    mid1_ref,
    turned1_ref,
    turned_in_ref,
    read_sems,
):
    reads = [
        pltpu.make_async_copy(source, target, read_sems.at[place])
        for place, (source, target) in enumerate(
            (
                (base_hbm, base_ref),
                (expand_hbm, expand_ref),
                (mid2_hbm, mid2_ref),
                (turned2_hbm, turned2_ref),
                (spatial_hbm, spatial_ref),
                (mid1_hbm, mid1_ref),
                (turned1_hbm, turned1_ref),
                (turned_in_hbm, turned_in_ref),
            )
        )
    ]
    for read in reads:
        read.start()
    side = 8
    rows, narrow = mid1_ref.shape
    wide = e_three.shape[1]
    crop_rows = rows // MICRO
    plane = side * side
    inverse = 1.0 / (MICRO * 64)
    scale = pooled_scale(where_ref[0] != 0, pool_ref, side * plane)

    reads[0].wait()
    step = 256
    for start in range(0, rows, step):
        crop = start // crop_rows
        for part in range(wide // LANES):
            lanes = slice(part * LANES, (part + 1) * LANES)
            at = slice(start, start + step)
            out_grad = out_grad_tile(scale, crop, part, base_ref[at, lanes])
            e_three[at, lanes] = (gain3_ref[:, lanes] * out_grad).astype(BF)

    for read in reads[1:4]:
        read.wait()
    expand_sum[...] = jnp.dot(turned2_ref[...], e_three[...], preferred_element_type=F32) * inverse

    for start in range(0, rows, crop_rows):
        at = slice(start, start + crop_rows)
        back = lax.dot_general(
            e_three[at, :], expand_ref[...], ROWS_BY_ROWS, preferred_element_type=F32
        )
        e_two = jnp.where(mid2_ref[at, :].astype(F32) > 0, gain2_ref[...] * back, 0.0)
        e_two = e_two.astype(BF).astype(F32).reshape(plane, side, narrow)
        place = lax.broadcasted_iota(jnp.int32, e_two.shape, 1)
        none = jnp.zeros((side, 1, side, narrow), F32)
        for off_c in (-1, 0, 1):
            if off_c == 0:
                moved = e_two
            elif off_c == 1:
                moved = jnp.where(place == 0, 0.0, pltpu.roll(e_two, 1, 1))
            else:
                moved = jnp.where(place == side - 1, 0.0, pltpu.roll(e_two, side - 1, 1))
            moved = moved.reshape(side, side, side, narrow)
            for off_b in (-1, 0, 1):
                if off_b == 0:
                    both = moved
                elif off_b == 1:
                    both = jnp.concatenate([none, moved[:, :-1]], axis=1)
                else:
                    both = jnp.concatenate([moved[:, 1:], none], axis=1)
                position = 3 * (off_b + 1) + (off_c + 1)
                shifts[at, position * narrow : (position + 1) * narrow] = both.reshape(
                    crop_rows, narrow
                ).astype(BF)

    for read in reads[4:6]:
        read.wait()
    empty = jnp.zeros((plane, narrow), F32)
    for crop in range(MICRO):
        at = slice(crop * crop_rows, (crop + 1) * crop_rows)
        spread = lax.dot_general(
            shifts[at, :], spatial_ref[...], ROWS_BY_ROWS, preferred_element_type=F32
        )
        lower = jnp.concatenate([spread[plane:, :narrow], empty], axis=0)
        upper = jnp.concatenate([empty, spread[:-plane, 2 * narrow :]], axis=0)
        back_one = lower + spread[:, narrow : 2 * narrow] + upper
        e_one_ref[at, :] = jnp.where(
            mid1_ref[at, :].astype(F32) > 0, gain1_ref[...] * back_one, 0.0
        ).astype(BF)

    for read in reads[6:]:
        read.wait()
    reduce_sum[...] = (
        jnp.dot(turned_in_ref[...], e_one_ref[...], preferred_element_type=F32) * inverse
    )

    for off_a in range(3):
        summed = (
            jnp.dot(
                turned1_ref[off_a * narrow : (off_a + 1) * narrow, :],
                shifts[...],
                preferred_element_type=F32,
            )
            * inverse
        )
        for position in range(9):
            block = off_a * 9 + position
            spatial_sum[block * narrow : (block + 1) * narrow, :] = summed[
                :, position * narrow : (position + 1) * narrow
            ]

    chips = 16
    height = kept_ref.shape[0] // chips
    chunk[140:144, :] = jnp.zeros((4, narrow), F32)

    def pack(chip, to, out_ref):
        for half in range(2):
            device = half * 2 * chips + chip * 2 + to
            chunk[half * 8 : half * 8 + 8, :] = reduce_sum[device * 8 : device * 8 + 8, :]
            for part in range(4):
                chunk[16 + half * 8 + part * 2 : 18 + half * 8 + part * 2, :] = expand_sum[
                    device * 2 : device * 2 + 2, part * LANES : (part + 1) * LANES
                ]
            chunk[32 + half * 54 : 86 + half * 54, :] = spatial_sum[
                device * 54 : device * 54 + 54, :
            ]
        out_ref[chip * height : (chip + 1) * height, :] = chunk[...].astype(BF)

    for core in range(2):

        @pl.when(where_ref[1] == core)
        def _(core=core):
            for chip in range(chips):
                pack(chip, core, kept_ref)
                pack(chip, 1 - core, given_ref)


def block_step(place, pool, base, mid1, mid2, turned1, turned2, turned_in, spatial, expand, gains):
    rows, narrow = mid1.shape
    wide = base.shape[1]
    smem = pl.BlockSpec(memory_space=pltpu.SMEM)
    vmem = pl.BlockSpec(memory_space=pltpu.VMEM)
    hbm = pl.BlockSpec(memory_space=pltpu.HBM)
    held = (base, expand, mid2, turned2, spatial, mid1, turned1, turned_in)
    return pl.pallas_call(
        block_kernel,
        out_shape=(
            jax.ShapeDtypeStruct((16 * 144, narrow), BF),
            jax.ShapeDtypeStruct((16 * 144, narrow), BF),
            jax.ShapeDtypeStruct((rows, narrow), BF),
        ),
        in_specs=[smem, vmem] + [hbm] * 8 + [vmem] * 3,
        out_specs=(vmem, vmem, vmem),
        scratch_shapes=[
            pltpu.VMEM((rows, wide), BF),
            pltpu.VMEM((rows, 9 * narrow), BF),
            pltpu.VMEM((27 * narrow, narrow), F32),
            pltpu.VMEM((narrow, wide), F32),
            pltpu.VMEM((wide, narrow), F32),
            pltpu.VMEM((144, narrow), F32),
        ]
        + [pltpu.VMEM(array.shape, BF) for array in held]
        + [pltpu.SemaphoreType.DMA((8,))],
        compiler_params=pltpu.CompilerParams(vmem_limit_bytes=VMEM_LIMIT),
        cost_estimate=pl.CostEstimate(
            flops=4_000_000_000, bytes_accessed=6_000_000, transcendentals=0
        ),
        name="block",
    )(
        place,
        pool,
        *in_hbm(base, mid1, mid2, turned1, turned2, turned_in, spatial, expand),
        *gains,
    )


def input_kernel(where_ref, pool_ref, base_ref, input_ref, e_one_ref, reduce_ref, out_ref):
    rows, wide = input_ref.shape
    crop_rows = rows // MICRO
    scale = pooled_scale(where_ref[0] != 0, pool_ref, crop_rows)
    step = 256
    for start in range(0, rows, step):
        at = slice(start, start + step)
        through = lax.dot_general(
            e_one_ref[at, :], reduce_ref[...], ROWS_BY_ROWS, preferred_element_type=F32
        )
        for part in range(wide // LANES):
            lanes = slice(part * LANES, (part + 1) * LANES)
            out_grad = out_grad_tile(scale, start // crop_rows, part, base_ref[at, lanes])
            out_ref[at, lanes] = jnp.where(
                input_ref[at, lanes].astype(F32) > 0, through[:, lanes] + out_grad, 0.0
            ).astype(BF)


def input_step(place, pool, base, input_pre, e_one, reduce):
    smem = pl.BlockSpec(memory_space=pltpu.SMEM)
    vmem = pl.BlockSpec(memory_space=pltpu.VMEM)
    return pl.pallas_call(
        input_kernel,
        out_shape=jax.ShapeDtypeStruct(input_pre.shape, BF),
        in_specs=[smem] + [vmem] * 5,
        out_specs=vmem,
        compiler_params=pltpu.CompilerParams(vmem_limit_bytes=VMEM_LIMIT),
        cost_estimate=pl.CostEstimate(
            flops=200_000_000, bytes_accessed=6_000_000, transcendentals=0
        ),
        name="input_grad",
    )(place, pool, base, input_pre, e_one, reduce)


def sum_kernel(half_ref, shares_ref, kept_ref, given_ref, total):
    height = total.shape[0]
    summed = shares_ref[0:height, :].astype(F32)
    for source in range(1, shares_ref.shape[0] // height):
        summed = summed + shares_ref[source * height : (source + 1) * height, :].astype(F32)
    total[...] = summed

    def put(target, half):
        target[0:8, :] = total[half * 8 : half * 8 + 8, :]
        target[8:16, :] = total[16 + half * 8 : 24 + half * 8, :]
        target[16:72, :] = total[32 + half * 54 : 88 + half * 54, :]

    @pl.when(half_ref[0] == 0)
    def _():
        put(kept_ref, 0)
        put(given_ref, 1)

    @pl.when(half_ref[0] != 0)
    def _():
        put(kept_ref, 1)
        put(given_ref, 0)


def sum_step(half, shares):
    smem = pl.BlockSpec(memory_space=pltpu.SMEM)
    vmem = pl.BlockSpec(memory_space=pltpu.VMEM)
    shape = jax.ShapeDtypeStruct((72, LANES), F32)
    return pl.pallas_call(
        sum_kernel,
        out_shape=(shape, shape),
        in_specs=[smem, vmem],
        out_specs=(vmem, vmem),
        scratch_shapes=[pltpu.VMEM((144, LANES), F32)],
        compiler_params=pltpu.CompilerParams(vmem_limit_bytes=VMEM_LIMIT),
        name="shares",
    )(half, shares)


def last_kernel(kept_ref, got_ref, reduce_ref, spatial_ref, expand_ref):
    total = kept_ref[...] + got_ref[...]
    reduce_ref[...] = total[0:8, :].astype(BF)
    spatial_ref[...] = total[16:70, :].astype(BF)
    expand_ref[...] = jnp.concatenate(
        [total[8 + 2 * part : 10 + 2 * part, :] for part in range(4)], axis=1
    ).astype(BF)


def last_step(kept, got):
    vmem = pl.BlockSpec(memory_space=pltpu.VMEM)
    return pl.pallas_call(
        last_kernel,
        out_shape=(
            jax.ShapeDtypeStruct((8, LANES), BF),
            jax.ShapeDtypeStruct((54, LANES), BF),
            jax.ShapeDtypeStruct((2, 4 * LANES), BF),
        ),
        in_specs=[vmem] * 2,
        out_specs=(vmem,) * 3,
        compiler_params=pltpu.CompilerParams(vmem_limit_bytes=2 * 1024 * 1024),
        name="weight_grads",
    )(kept, got)


def copies(shard, count):
    rows, width = shard.shape
    return jnp.broadcast_to(shard[None], (count, rows, width)).reshape(count * rows, width)


def in_hbm(*arrays):
    return [pltpu.with_memory_space_constraint(array, pltpu.HBM) for array in arrays]


def shards(
    projections,
    partner,
    plan,
    head_pre,
    head_in,
    head_out,
    final_pre,
    incoming,
    input_pre,
    mid_pre1,
    mid_pre2,
    w_reduce,
    w_spatial,
    w_expand,
    gain1,
    gain2,
    gain3,
):
    row_count = projections.shape[0]
    sections = lax.axis_size("section")
    peers = lax.axis_size(PLANE)
    upper = lax.axis_index("z_hi")
    me = lax.axis_index(PLANE)
    swap_near = [
        (half * sections + s, (1 - half) * sections + (s + sections // 2) % sections)
        for half in range(2)
        for s in range(sections)
    ]
    swap_far = [(0, 1), (1, 0)]
    narrow = w_reduce.shape[2]
    wide = w_expand.shape[2]
    core = lax.axis_index("core")
    section = lax.axis_index("section")
    chips = peers // 2
    other_rows = lax.ppermute(projections, ("z_hi", "section"), swap_near)
    n_reduce, n_spatial = w_reduce.shape[1], w_spatial.shape[1]
    n_expand = w_expand.shape[1] * wide // narrow
    packed = jnp.concatenate(
        [
            w_reduce[0],
            w_expand[0].reshape(n_expand, narrow),
            w_spatial[0],
            w_reduce[0, : 72 - n_reduce - n_expand - n_spatial],
        ],
        axis=0,
    )
    flat_one = mid_pre1.reshape(-1, narrow)
    flat_two = mid_pre2.reshape(-1, narrow)
    flat_in = input_pre.reshape(-1, wide)
    is_last = section == sections - 1
    place = jnp.stack([is_last.astype(jnp.int32), core.astype(jnp.int32)])
    sent, packed = lax.optimization_barrier(
        (copies(jnp.concatenate([projections, other_rows], axis=0), chips), packed)
    )
    near = lax.all_to_all(sent, ("x", "y"), 0, 0, tiled=True)
    far = lax.ppermute(packed, "z_hi", swap_far)
    ordered = jnp.where(
        upper == 0,
        jnp.concatenate([packed, far], axis=0),
        jnp.concatenate([far, packed], axis=0),
    )
    near, weights = lax.optimization_barrier((near, copies(ordered, chips)))
    across = lax.ppermute(near, "core", swap_far)
    half_crops = peers * row_count
    partner_device = partner % half_crops // row_count
    partner_row = (
        jnp.where(partner_device % 2 == core, 0, half_crops)
        + partner_device // 2 * (2 * row_count)
        + jnp.where(partner // half_crops == upper, 0, row_count)
        + partner % row_count
    )

    weights_near = lax.all_to_all(weights, ("x", "y"), 0, 0, tiled=True)
    projection_gradient, pool_copies = loss_step(
        (me // 2 * 2 * row_count).reshape(1),
        plan,
        near,
        across,
        partner_row.reshape(-1, 1),
        head_pre,
        head_in,
        head_out,
        row_count,
        sections,
    )
    pool = lax.all_to_all(pool_copies, "section", 0, 0, tiled=True)
    weights_near, pool_copies = lax.optimization_barrier((weights_near, pool_copies))
    weights_across = lax.ppermute(weights_near, "core", swap_far)
    turned_one, turned_two, turned_in, base, full_spatial, full_expand, full_reduce = prepare_step(
        place,
        weights_near,
        weights_across,
        final_pre.reshape(-1, wide),
        incoming.reshape(-1, wide),
        flat_one,
        flat_two,
        flat_in,
    )
    kept, given, e_one = block_step(
        place,
        pool,
        base,
        flat_one,
        flat_two,
        turned_one,
        turned_two,
        turned_in,
        full_spatial,
        full_expand,
        (gain1, gain2, gain3),
    )
    got = lax.ppermute(given, "core", swap_far)
    paired = (kept.astype(F32) + got.astype(F32)).astype(BF)
    shares = lax.all_to_all(paired, ("x", "y"), 0, 0, tiled=True)
    input_grad = input_step(place, pool, base, flat_in, e_one, full_reduce)
    kept, given = sum_step(upper.astype(jnp.int32).reshape(1), shares)
    got = lax.ppermute(given, "z_hi", swap_far)
    sum_reduce, sum_spatial, sum_expand = last_step(kept, got)
    return (
        projection_gradient,
        input_grad.reshape(input_pre.shape),
        sum_reduce[None],
        sum_spatial[None],
        sum_expand[None],
    )


def solution(mesh):
    fine = Mesh(
        mesh.devices.reshape(2, 4, 4, 2, mesh.shape["section"]),
        ("z_hi", "x", "y", "core", "section"),
    )
    placed = (
        P(DP, None),
        P(DP),
        P(DP, None),
        P(DP, "section"),
        P(None, "section"),
        P("section", None),
        P(DP, None, None, None, None),
        P("section", DP, None, None, None, None),
        P("section", DP, None, None, None, None),
        P("section", DP, None, None, None, None),
        P("section", DP, None, None, None, None),
        P("section", DP, None),
        P("section", DP, None),
        P("section", DP, None),
        P("section", None),
        P("section", None),
        P("section", None),
    )
    return jax.shard_map(
        shards,
        mesh=fine,
        in_specs=placed,
        out_specs=(
            P(DP, None),
            P("section", DP, None, None, None, None),
            P("section", DP, None),
            P("section", DP, None),
            P("section", DP, None),
        ),
        check_vma=False,
    )
```

```python
import functools

import jax
import jax.numpy as jnp
from jax import lax
from jax.experimental import pallas as pl
from jax.experimental.pallas import tpu as pltpu
from jax.sharding import Mesh
from jax.sharding import PartitionSpec as P

MICRO = 2
SOFTMAX_TEMP = 0.5
LOSS_SCALE = 1024.0
PLANE = ("x", "y", "core")
DP = ("z_hi", "x", "y", "core")
LANES = 128
TILE = 256
BF = jnp.bfloat16
F32 = jnp.float32
ROWS_BY_ROWS = (((1,), (1,)), ((), ()))
VMEM_LIMIT = 24 * 1024 * 1024


def three_parts(values):
    high = values.astype(BF)
    rest = values - high.astype(F32)
    middle = rest.astype(BF)
    return high, middle, (rest - middle.astype(F32)).astype(BF)


def prepare_kernel(
    where_ref,
    final_hbm,
    incoming_hbm,
    mid1_hbm,
    mid2_hbm,
    input_hbm,
    one_hbm,
    two_ref,
    in_hbm,
    base_ref,
    final_ref,
    mid1_ref,
    mid2_ref,
    input_ref,
    one_ref,
    in_ref,
    read_sems,
    write_sems,
):
    rows, narrow = mid1_ref.shape
    wide = input_ref.shape[1]
    crop_rows = rows // MICRO
    reads = [
        pltpu.make_async_copy(source, target, read_sems.at[place])
        for place, (source, target) in enumerate(
            ((mid1_hbm, mid1_ref), (mid2_hbm, mid2_ref), (input_hbm, input_ref))
        )
    ]
    for read in reads:
        read.start()
    write_one = pltpu.make_async_copy(one_ref, one_hbm, write_sems.at[0])
    write_in = pltpu.make_async_copy(in_ref, in_hbm, write_sems.at[1])
    empty = jnp.zeros((64, narrow), BF)
    reads[0].wait()
    for crop in range(MICRO):
        at = slice(crop * crop_rows, (crop + 1) * crop_rows)
        hidden = jnp.maximum(mid1_ref[at, :], 0)
        moved = (
            jnp.concatenate([empty, hidden[:-64]], axis=0),
            hidden,
            jnp.concatenate([hidden[64:], empty], axis=0),
        )
        for off_a in range(3):
            one_ref[off_a * narrow : (off_a + 1) * narrow, at] = moved[off_a].T
    write_one.start()
    reads[1].wait()
    two_ref[...] = jnp.maximum(mid2_ref[...], 0).T
    reads[2].wait()
    for part in range(wide // LANES):
        lanes = slice(part * LANES, (part + 1) * LANES)
        in_ref[lanes, :] = jnp.maximum(input_ref[:, lanes], 0).T
    write_in.start()

    @pl.when(where_ref[0] != 0)
    def _():
        read = pltpu.make_async_copy(final_hbm, final_ref, read_sems.at[3])
        read.start()
        read.wait()
        base_ref[...] = jnp.where(final_ref[...].astype(F32) > 0, 1.0, 0.0).astype(BF)

    @pl.when(where_ref[0] == 0)
    def _():
        read = pltpu.make_async_copy(incoming_hbm, base_ref, read_sems.at[3])
        read.start()
        read.wait()

    write_one.wait()
    write_in.wait()


def prepare_step(place, final, incoming, mid1, mid2, input_pre):
    rows, narrow = mid1.shape
    wide = input_pre.shape[1]
    smem = pl.BlockSpec(memory_space=pltpu.SMEM)
    hbm = pl.BlockSpec(memory_space=pltpu.HBM)
    vmem = pl.BlockSpec(memory_space=pltpu.VMEM)
    held = (final.shape, mid1.shape, mid2.shape, input_pre.shape)
    turned = ((3 * narrow, rows), (wide, rows))
    return pl.pallas_call(
        prepare_kernel,
        out_shape=(
            pltpu.HBM(turned[0], BF),
            pltpu.VMEM((narrow, rows), BF),
            pltpu.HBM(turned[1], BF),
            pltpu.VMEM((rows, wide), BF),
        ),
        in_specs=[smem] + [hbm] * 5,
        out_specs=(hbm, vmem, hbm, vmem),
        scratch_shapes=[pltpu.VMEM(shape, BF) for shape in (*held, *turned)]
        + [pltpu.SemaphoreType.DMA((4,)), pltpu.SemaphoreType.DMA((2,))],
        compiler_params=pltpu.CompilerParams(vmem_limit_bytes=VMEM_LIMIT),
        cost_estimate=pl.CostEstimate(flops=0, bytes_accessed=6_000_000, transcendentals=0),
        name="prepare",
    )(place, *in_hbm(final, incoming, mid1, mid2, input_pre))


def unpack_kernel(
    where_ref,
    near_ref,
    across_ref,
    spatial_ref,
    expand_ref,
    reduce_ref,
    spatial_rows,
    expand_rows,
    reduce_rows,
):
    narrow = near_ref.shape[1]
    chips = near_ref.shape[0] // 144

    def unpack(source, chip, core):
        shard = source[chip * 144 : (chip + 1) * 144, :].astype(F32)
        for half in range(2):
            device = half * 2 * chips + chip * 2 + core
            top = half * 72
            reduce_rows[device * 8 : device * 8 + 8, :] = shard[top : top + 8]
            for part in range(8):
                row, lane = device * 2 + part // 4, part % 4 * LANES
                expand_rows[row : row + 1, lane : lane + LANES] = shard[
                    top + 8 + part : top + 9 + part
                ]
            spatial_rows[device * 54 : device * 54 + 54, :] = shard[top + 16 : top + 70]

    for core in range(2):

        @pl.when(where_ref[1] == core)
        def _(core=core):
            for chip in range(chips):
                unpack(near_ref, chip, core)
                unpack(across_ref, chip, 1 - core)

    reduce_ref[...] = reduce_rows[...].astype(BF)
    expand_ref[...] = expand_rows[...].astype(BF)
    for off_a in range(3):
        for position in range(9):
            block = off_a * 9 + position
            spatial_ref[
                off_a * narrow : (off_a + 1) * narrow, position * narrow : (position + 1) * narrow
            ] = spatial_rows[block * narrow : (block + 1) * narrow, :].astype(BF)


def unpack_step(place, near, across, wide):
    narrow = near.shape[1]
    smem = pl.BlockSpec(memory_space=pltpu.SMEM)
    vmem = pl.BlockSpec(memory_space=pltpu.VMEM)
    outs = ((3 * narrow, 9 * narrow), (narrow, wide), (wide, narrow))
    return pl.pallas_call(
        unpack_kernel,
        out_shape=(
            pltpu.VMEM(outs[0], BF),
            pltpu.VMEM(outs[1], BF),
            jax.ShapeDtypeStruct(outs[2], BF),
        ),
        in_specs=[smem] + [vmem] * 2,
        out_specs=(vmem,) * 3,
        scratch_shapes=[
            pltpu.VMEM((27 * narrow, narrow), F32),
            pltpu.VMEM((narrow, wide), F32),
            pltpu.VMEM((wide, narrow), F32),
        ],
        compiler_params=pltpu.CompilerParams(vmem_limit_bytes=VMEM_LIMIT),
        cost_estimate=pl.CostEstimate(flops=0, bytes_accessed=3_000_000, transcendentals=0),
        name="unpack",
    )(place, *in_vmem(near, across))


def loss_kernel(
    where_ref,
    plan_ref,
    near_ref,
    across_ref,
    partner_ref,
    head_pre_ref,
    head_in_ref,
    head_out_ref,
    grad_ref,
    pool_ref,
    left,
    right,
    even,
    odd,
    totals,
):
    crops = left.shape[0]
    own = grad_ref.shape[0]
    tiles = crops // TILE
    first = pl.multiple_of(where_ref[0], own)

    for half, rows_ref in enumerate((near_ref, across_ref)):
        count = rows_ref.shape[0]

        def split(r, _, half=half, rows_ref=rows_ref, count=count):
            a, b, c = three_parts(rows_ref[pl.ds(pl.multiple_of(r * TILE, TILE), TILE), :])
            at = pl.ds(pl.multiple_of(half * count + r * TILE, TILE), TILE)
            a2, b2, c2 = a * 2, b * 2, c * 2
            for place, part in enumerate((a2, b2, a2, b2, a2, c2)):
                left[at, place * LANES : (place + 1) * LANES] = part
            for place, part in enumerate((a, a, b, b, c, a)):
                right[at, place * LANES : (place + 1) * LANES] = part
            return 0

        lax.fori_loop(0, count // TILE, split, 0)

    diagonal = lax.broadcasted_iota(jnp.int32, (TILE, TILE), 0) == lax.broadcasted_iota(
        jnp.int32, (TILE, TILE), 1
    )
    groups = crops // 8

    def score_block(j, scores):
        at = pl.ds(pl.multiple_of(j * TILE, TILE), TILE)
        scores[...] = lax.dot_general(
            left[...], right[at, :], ROWS_BY_ROWS, preferred_element_type=F32
        )
        scores[at, :] = jnp.where(diagonal, -jnp.inf, scores[at, :])
        largest = jnp.max(scores[...].reshape(groups, 8, TILE), axis=0)
        return jnp.broadcast_to(jnp.max(largest, axis=0, keepdims=True), (8, TILE))

    def sum_block(j, scores, largest):
        at = pl.ds(pl.multiple_of(j * TILE, TILE), TILE)
        summed = jnp.sum(jnp.exp(scores[...].reshape(groups, 8, TILE) - largest[None]), axis=0)
        whole = jnp.broadcast_to(jnp.sum(summed, axis=0, keepdims=True), (8, TILE))
        totals[:, at] = largest + jnp.log(whole)

    def two_blocks(pair, largest):
        j = 2 * pair
        following = score_block(j + 1, odd)
        sum_block(j, even, largest)
        after = score_block(j + 2, even)
        sum_block(j + 1, odd, following)
        return after

    largest = lax.fori_loop(0, tiles // 2 - 1, two_blocks, score_block(0, even))
    following = score_block(tiles - 1, odd)
    sum_block(tiles - 2, even, largest)
    sum_block(tiles - 1, odd, following)

    mine = lax.dot_general(
        left[pl.ds(first, own), :], right[...], ROWS_BY_ROWS, preferred_element_type=F32
    )
    columns = lax.broadcasted_iota(jnp.int32, (own, crops), 1)
    mine = jnp.where(
        columns == lax.broadcasted_iota(jnp.int32, (own, crops), 0) + first, -jnp.inf, mine
    )
    peak = jnp.max(mine, axis=1, keepdims=True)
    my_totals = peak + jnp.log(jnp.sum(jnp.exp(mine - peak), axis=1, keepdims=True))
    blended = jnp.exp(mine - my_totals) + jnp.exp(mine - totals[0:1, :])
    blended = blended - jnp.where(columns == partner_ref[...], 2.0, 0.0)
    a, b, c = three_parts(blended)
    stacked = jnp.concatenate([a, b, c], axis=0)
    products = jnp.dot(stacked, right[:, LANES : 3 * LANES], preferred_element_type=F32)
    low = jnp.dot(a, right[:, 4 * LANES : 5 * LANES], preferred_element_type=F32)
    small = products[own : 2 * own, LANES:] + products[2 * own :, :LANES] + low
    gradient = (
        products[:own, :LANES] + (products[:own, LANES:] + products[own : 2 * own, :LANES] + small)
    ) / SOFTMAX_TEMP
    grad_ref[...] = gradient

    pick_row = lax.broadcasted_iota(jnp.int32, (16, own), 0)
    pick_column = lax.broadcasted_iota(jnp.int32, (16, own), 1)
    wanted = jnp.where(pick_row == 0, plan_ref[0, 0], plan_ref[0, 1])
    chosen = jnp.where((pick_column == wanted) & (pick_row < MICRO), 1.0, 0.0).astype(BF)
    picked = jnp.dot(chosen, gradient.astype(BF), preferred_element_type=F32).astype(BF)
    hid_back = lax.dot_general(
        picked, head_out_ref[...], ROWS_BY_ROWS, preferred_element_type=F32
    )
    hid_grad = jnp.where(head_pre_ref[...].astype(F32) > 0, hid_back[:MICRO], 0.0)
    hid_grad = jnp.concatenate(
        [hid_grad, jnp.zeros((16 - MICRO, hid_grad.shape[1]), F32)], axis=0
    ).astype(BF)
    pool = lax.dot_general(hid_grad, head_in_ref[...], ROWS_BY_ROWS, preferred_element_type=F32)
    parts = pool.shape[1] // LANES
    packed = jnp.concatenate(
        [pool[m : m + 1, n * LANES : (n + 1) * LANES] for m in range(MICRO) for n in range(parts)],
        axis=0,
    )
    for copy in range(pool_ref.shape[0] // packed.shape[0]):
        pool_ref[copy * packed.shape[0] : (copy + 1) * packed.shape[0], :] = packed


def loss_step(first_row, plan, near, across, partner_row, head_pre, head_in, head_out, own, sections):
    crops, width = 2 * near.shape[0], near.shape[1]
    pool_rows = MICRO * head_in.shape[0] // LANES
    smem = pl.BlockSpec(memory_space=pltpu.SMEM)
    vmem = pl.BlockSpec(memory_space=pltpu.VMEM)
    return pl.pallas_call(
        loss_kernel,
        out_shape=(
            jax.ShapeDtypeStruct((own, width), F32),
            jax.ShapeDtypeStruct((sections * pool_rows, LANES), F32),
        ),
        in_specs=[smem, smem] + [vmem] * 6,
        out_specs=(vmem, vmem),
        scratch_shapes=[
            pltpu.VMEM((crops, 6 * LANES), BF),
            pltpu.VMEM((crops, 6 * LANES), BF),
            pltpu.VMEM((crops, TILE), F32),
            pltpu.VMEM((crops, TILE), F32),
            pltpu.VMEM((8, crops), F32),
        ],
        compiler_params=pltpu.CompilerParams(vmem_limit_bytes=VMEM_LIMIT),
        cost_estimate=pl.CostEstimate(
            flops=12_000_000_000, bytes_accessed=2_000_000, transcendentals=4_000_000
        ),
        name="loss",
    )(first_row, plan, *in_vmem(near, across), partner_row, head_pre, head_in, head_out)


def pooled_scale(last, pool_ref, voxels):
    rows = MICRO * 4
    total = pool_ref[0:rows, :]
    for source in range(1, pool_ref.shape[0] // rows):
        total = total + pool_ref[source * rows : (source + 1) * rows, :]
    return jnp.where(last, total * (LOSS_SCALE / voxels), 1.0)


def out_grad_tile(scale, crop, part, base):
    return base.astype(F32) * scale[crop * 4 + part : crop * 4 + part + 1, :]


def block_kernel(
    where_ref,
    pool_ref,
    base_ref,
    mid1_hbm,
    mid2_hbm,
    turned1_hbm,
    turned2_ref,
    turned_in_hbm,
    spatial_ref,
    expand_ref,
    gain1_ref,
    gain2_ref,
    gain3_ref,
    kept_ref,
    given_ref,
    e_one_ref,
    e_three,
    shifts,
    spatial_sum,
    expand_sum,
    reduce_sum,
    chunk,
    mid1_ref,
    mid2_ref,
    turned1_ref,
    turned_in_ref,
    read_sems,
):
    reads = [
        pltpu.make_async_copy(mid2_hbm, mid2_ref, read_sems.at[0]),
        pltpu.make_async_copy(mid1_hbm, mid1_ref, read_sems.at[1]),
        pltpu.make_async_copy(turned_in_hbm, turned_in_ref, read_sems.at[2]),
        pltpu.make_async_copy(turned1_hbm, turned1_ref, read_sems.at[3]),
    ]
    for read in reads:
        read.start()
    side = 8
    rows, narrow = mid1_ref.shape
    wide = e_three.shape[1]
    crop_rows = rows // MICRO
    plane = side * side
    inverse = 1.0 / (MICRO * 64)
    scale = pooled_scale(where_ref[0] != 0, pool_ref, side * plane)

    step = 256
    for start in range(0, rows, step):
        crop = start // crop_rows
        for part in range(wide // LANES):
            lanes = slice(part * LANES, (part + 1) * LANES)
            at = slice(start, start + step)
            out_grad = out_grad_tile(scale, crop, part, base_ref[at, lanes])
            e_three[at, lanes] = (gain3_ref[:, lanes] * out_grad).astype(BF)

    expand_sum[...] = jnp.dot(turned2_ref[...], e_three[...], preferred_element_type=F32) * inverse
    reads[0].wait()

    for start in range(0, rows, crop_rows):
        at = slice(start, start + crop_rows)
        back = lax.dot_general(
            e_three[at, :], expand_ref[...], ROWS_BY_ROWS, preferred_element_type=F32
        )
        e_two = jnp.where(mid2_ref[at, :].astype(F32) > 0, gain2_ref[...] * back, 0.0)
        e_two = e_two.astype(BF).astype(F32).reshape(plane, side, narrow)
        place = lax.broadcasted_iota(jnp.int32, e_two.shape, 1)
        none = jnp.zeros((side, 1, side, narrow), F32)
        for off_c in (-1, 0, 1):
            if off_c == 0:
                moved = e_two
            elif off_c == 1:
                moved = jnp.where(place == 0, 0.0, pltpu.roll(e_two, 1, 1))
            else:
                moved = jnp.where(place == side - 1, 0.0, pltpu.roll(e_two, side - 1, 1))
            moved = moved.reshape(side, side, side, narrow)
            for off_b in (-1, 0, 1):
                if off_b == 0:
                    both = moved
                elif off_b == 1:
                    both = jnp.concatenate([none, moved[:, :-1]], axis=1)
                else:
                    both = jnp.concatenate([moved[:, 1:], none], axis=1)
                position = 3 * (off_b + 1) + (off_c + 1)
                shifts[at, position * narrow : (position + 1) * narrow] = both.reshape(
                    crop_rows, narrow
                ).astype(BF)

    reads[1].wait()
    empty = jnp.zeros((plane, narrow), F32)
    for crop in range(MICRO):
        at = slice(crop * crop_rows, (crop + 1) * crop_rows)
        spread = lax.dot_general(
            shifts[at, :], spatial_ref[...], ROWS_BY_ROWS, preferred_element_type=F32
        )
        lower = jnp.concatenate([spread[plane:, :narrow], empty], axis=0)
        upper = jnp.concatenate([empty, spread[:-plane, 2 * narrow :]], axis=0)
        back_one = lower + spread[:, narrow : 2 * narrow] + upper
        e_one_ref[at, :] = jnp.where(
            mid1_ref[at, :].astype(F32) > 0, gain1_ref[...] * back_one, 0.0
        ).astype(BF)

    reads[2].wait()
    reduce_sum[...] = (
        jnp.dot(turned_in_ref[...], e_one_ref[...], preferred_element_type=F32) * inverse
    )

    reads[3].wait()
    for off_a in range(3):
        summed = (
            jnp.dot(
                turned1_ref[off_a * narrow : (off_a + 1) * narrow, :],
                shifts[...],
                preferred_element_type=F32,
            )
            * inverse
        )
        for position in range(9):
            block = off_a * 9 + position
            spatial_sum[block * narrow : (block + 1) * narrow, :] = summed[
                :, position * narrow : (position + 1) * narrow
            ]

    chips = 16
    height = kept_ref.shape[0] // chips
    chunk[140:144, :] = jnp.zeros((4, narrow), F32)

    def pack(chip, to, out_ref):
        for half in range(2):
            device = half * 2 * chips + chip * 2 + to
            chunk[half * 8 : half * 8 + 8, :] = reduce_sum[device * 8 : device * 8 + 8, :]
            for part in range(4):
                chunk[16 + half * 8 + part * 2 : 18 + half * 8 + part * 2, :] = expand_sum[
                    device * 2 : device * 2 + 2, part * LANES : (part + 1) * LANES
                ]
            chunk[32 + half * 54 : 86 + half * 54, :] = spatial_sum[
                device * 54 : device * 54 + 54, :
            ]
        out_ref[chip * height : (chip + 1) * height, :] = chunk[...].astype(BF)

    for core in range(2):

        @pl.when(where_ref[1] == core)
        def _(core=core):
            for chip in range(chips):
                pack(chip, core, kept_ref)
                pack(chip, 1 - core, given_ref)


def block_step(place, pool, base, mid1, mid2, turned1, turned2, turned_in, spatial, expand, gains):
    rows, narrow = mid1.shape
    wide = base.shape[1]
    smem = pl.BlockSpec(memory_space=pltpu.SMEM)
    vmem = pl.BlockSpec(memory_space=pltpu.VMEM)
    hbm = pl.BlockSpec(memory_space=pltpu.HBM)
    return pl.pallas_call(
        block_kernel,
        out_shape=(
            jax.ShapeDtypeStruct((16 * 144, narrow), BF),
            jax.ShapeDtypeStruct((16 * 144, narrow), BF),
            jax.ShapeDtypeStruct((rows, narrow), BF),
        ),
        in_specs=[smem, vmem, vmem, hbm, hbm, hbm, vmem, hbm] + [vmem] * 5,
        out_specs=(vmem, vmem, vmem),
        scratch_shapes=[
            pltpu.VMEM((rows, wide), BF),
            pltpu.VMEM((rows, 9 * narrow), BF),
            pltpu.VMEM((27 * narrow, narrow), F32),
            pltpu.VMEM((narrow, wide), F32),
            pltpu.VMEM((wide, narrow), F32),
            pltpu.VMEM((144, narrow), F32),
        ]
        + [pltpu.VMEM(array.shape, BF) for array in (mid1, mid2, turned1, turned_in)]
        + [pltpu.SemaphoreType.DMA((4,))],
        compiler_params=pltpu.CompilerParams(vmem_limit_bytes=VMEM_LIMIT),
        cost_estimate=pl.CostEstimate(
            flops=4_000_000_000, bytes_accessed=6_000_000, transcendentals=0
        ),
        name="block",
    )(
        place,
        pool,
        *in_vmem(base),
        *in_hbm(mid1, mid2, turned1),
        *in_vmem(turned2),
        *in_hbm(turned_in),
        *in_vmem(spatial, expand),
        *gains,
    )


def input_kernel(where_ref, pool_ref, base_ref, input_ref, e_one_ref, reduce_ref, out_ref):
    rows, wide = input_ref.shape
    crop_rows = rows // MICRO
    scale = pooled_scale(where_ref[0] != 0, pool_ref, crop_rows)
    step = 256
    for start in range(0, rows, step):
        at = slice(start, start + step)
        through = lax.dot_general(
            e_one_ref[at, :], reduce_ref[...], ROWS_BY_ROWS, preferred_element_type=F32
        )
        for part in range(wide // LANES):
            lanes = slice(part * LANES, (part + 1) * LANES)
            out_grad = out_grad_tile(scale, start // crop_rows, part, base_ref[at, lanes])
            out_ref[at, lanes] = jnp.where(
                input_ref[at, lanes].astype(F32) > 0, through[:, lanes] + out_grad, 0.0
            ).astype(BF)


def input_step(place, pool, base, input_pre, e_one, reduce):
    smem = pl.BlockSpec(memory_space=pltpu.SMEM)
    vmem = pl.BlockSpec(memory_space=pltpu.VMEM)
    return pl.pallas_call(
        input_kernel,
        out_shape=jax.ShapeDtypeStruct(input_pre.shape, BF),
        in_specs=[smem] + [vmem] * 5,
        out_specs=vmem,
        compiler_params=pltpu.CompilerParams(vmem_limit_bytes=VMEM_LIMIT),
        cost_estimate=pl.CostEstimate(
            flops=200_000_000, bytes_accessed=6_000_000, transcendentals=0
        ),
        name="input_grad",
    )(place, pool, base, input_pre, e_one, reduce)


def sum_kernel(half_ref, shares_ref, kept_ref, given_ref, total):
    height = total.shape[0]
    summed = shares_ref[0:height, :].astype(F32)
    for source in range(1, shares_ref.shape[0] // height):
        summed = summed + shares_ref[source * height : (source + 1) * height, :].astype(F32)
    total[...] = summed

    def put(target, half):
        target[0:8, :] = total[half * 8 : half * 8 + 8, :]
        target[8:16, :] = total[16 + half * 8 : 24 + half * 8, :]
        target[16:72, :] = total[32 + half * 54 : 88 + half * 54, :]

    @pl.when(half_ref[0] == 0)
    def _():
        put(kept_ref, 0)
        put(given_ref, 1)

    @pl.when(half_ref[0] != 0)
    def _():
        put(kept_ref, 1)
        put(given_ref, 0)


def sum_step(half, shares):
    smem = pl.BlockSpec(memory_space=pltpu.SMEM)
    vmem = pl.BlockSpec(memory_space=pltpu.VMEM)
    shape = jax.ShapeDtypeStruct((72, LANES), F32)
    return pl.pallas_call(
        sum_kernel,
        out_shape=(shape, shape),
        in_specs=[smem, vmem],
        out_specs=(vmem, vmem),
        scratch_shapes=[pltpu.VMEM((144, LANES), F32)],
        compiler_params=pltpu.CompilerParams(vmem_limit_bytes=VMEM_LIMIT),
        name="shares",
    )(half, shares)


def last_kernel(kept_ref, got_ref, reduce_ref, spatial_ref, expand_ref):
    total = kept_ref[...] + got_ref[...]
    reduce_ref[...] = total[0:8, :].astype(BF)
    spatial_ref[...] = total[16:70, :].astype(BF)
    expand_ref[...] = jnp.concatenate(
        [total[8 + 2 * part : 10 + 2 * part, :] for part in range(4)], axis=1
    ).astype(BF)


def last_step(kept, got):
    vmem = pl.BlockSpec(memory_space=pltpu.VMEM)
    return pl.pallas_call(
        last_kernel,
        out_shape=(
            jax.ShapeDtypeStruct((8, LANES), BF),
            jax.ShapeDtypeStruct((54, LANES), BF),
            jax.ShapeDtypeStruct((2, 4 * LANES), BF),
        ),
        in_specs=[vmem] * 2,
        out_specs=(vmem,) * 3,
        compiler_params=pltpu.CompilerParams(vmem_limit_bytes=2 * 1024 * 1024),
        name="weight_grads",
    )(kept, got)


def copies(shard, count):
    rows, width = shard.shape
    return jnp.broadcast_to(shard[None], (count, rows, width)).reshape(count * rows, width)


def in_vmem(*arrays):
    return [pltpu.with_memory_space_constraint(array, pltpu.VMEM) for array in arrays]


def in_hbm(*arrays):
    return [pltpu.with_memory_space_constraint(array, pltpu.HBM) for array in arrays]


def shards(
    projections,
    partner,
    plan,
    head_pre,
    head_in,
    head_out,
    final_pre,
    incoming,
    input_pre,
    mid_pre1,
    mid_pre2,
    w_reduce,
    w_spatial,
    w_expand,
    gain1,
    gain2,
    gain3,
):
    row_count = projections.shape[0]
    sections = lax.axis_size("section")
    peers = lax.axis_size(PLANE)
    upper = lax.axis_index("z_hi")
    me = lax.axis_index(PLANE)
    swap_near = [
        (half * sections + s, (1 - half) * sections + (s + sections // 2) % sections)
        for half in range(2)
        for s in range(sections)
    ]
    swap_far = [(0, 1), (1, 0)]
    narrow = w_reduce.shape[2]
    wide = w_expand.shape[2]
    core = lax.axis_index("core")
    section = lax.axis_index("section")
    chips = peers // 2
    other_rows = lax.ppermute(projections, ("z_hi", "section"), swap_near)
    n_reduce, n_spatial = w_reduce.shape[1], w_spatial.shape[1]
    n_expand = w_expand.shape[1] * wide // narrow
    packed = jnp.concatenate(
        [
            w_reduce[0],
            w_expand[0].reshape(n_expand, narrow),
            w_spatial[0],
            w_reduce[0, : 72 - n_reduce - n_expand - n_spatial],
        ],
        axis=0,
    )
    flat_one = mid_pre1.reshape(-1, narrow)
    flat_two = mid_pre2.reshape(-1, narrow)
    flat_in = input_pre.reshape(-1, wide)
    is_last = section == sections - 1
    place = jnp.stack([is_last.astype(jnp.int32), core.astype(jnp.int32)])
    sent, packed = lax.optimization_barrier(
        (copies(jnp.concatenate([projections, other_rows], axis=0), chips), packed)
    )
    near = lax.all_to_all(sent, ("x", "y"), 0, 0, tiled=True)
    far = lax.ppermute(packed, "z_hi", swap_far)
    ordered = jnp.where(
        upper == 0,
        jnp.concatenate([packed, far], axis=0),
        jnp.concatenate([far, packed], axis=0),
    )
    near, weights = lax.optimization_barrier((near, copies(ordered, chips)))
    across = lax.ppermute(near, "core", swap_far)
    half_crops = peers * row_count
    partner_device = partner % half_crops // row_count
    partner_row = (
        jnp.where(partner_device % 2 == core, 0, half_crops)
        + partner_device // 2 * (2 * row_count)
        + jnp.where(partner // half_crops == upper, 0, row_count)
        + partner % row_count
    )

    weights_near = lax.all_to_all(weights, ("x", "y"), 0, 0, tiled=True)
    projection_gradient, pool_copies = loss_step(
        (me // 2 * 2 * row_count).reshape(1),
        plan,
        near,
        across,
        partner_row.reshape(-1, 1),
        head_pre,
        head_in,
        head_out,
        row_count,
        sections,
    )
    pool = lax.all_to_all(pool_copies, "section", 0, 0, tiled=True)
    weights_near, pool_copies = lax.optimization_barrier((weights_near, pool_copies))
    weights_across = lax.ppermute(weights_near, "core", swap_far)
    place, weights_across = lax.optimization_barrier((place, weights_across))
    turned_one, turned_two, turned_in, base = prepare_step(
        place,
        final_pre.reshape(-1, wide),
        incoming.reshape(-1, wide),
        flat_one,
        flat_two,
        flat_in,
    )
    full_spatial, full_expand, full_reduce = unpack_step(
        place, weights_near, weights_across, wide
    )
    kept, given, e_one = block_step(
        place,
        pool,
        base,
        flat_one,
        flat_two,
        turned_one,
        turned_two,
        turned_in,
        full_spatial,
        full_expand,
        (gain1, gain2, gain3),
    )
    got = lax.ppermute(given, "core", swap_far)
    paired = (kept.astype(F32) + got.astype(F32)).astype(BF)
    shares = lax.all_to_all(paired, ("x", "y"), 0, 0, tiled=True)
    input_grad = input_step(place, pool, base, flat_in, e_one, full_reduce)
    kept, given = sum_step(upper.astype(jnp.int32).reshape(1), shares)
    got = lax.ppermute(given, "z_hi", swap_far)
    sum_reduce, sum_spatial, sum_expand = last_step(kept, got)
    return (
        projection_gradient,
        input_grad.reshape(input_pre.shape),
        sum_reduce[None],
        sum_spatial[None],
        sum_expand[None],
    )


def solution(mesh):
    fine = Mesh(
        mesh.devices.reshape(2, 4, 4, 2, mesh.shape["section"]),
        ("z_hi", "x", "y", "core", "section"),
    )
    placed = (
        P(DP, None),
        P(DP),
        P(DP, None),
        P(DP, "section"),
        P(None, "section"),
        P("section", None),
        P(DP, None, None, None, None),
        P("section", DP, None, None, None, None),
        P("section", DP, None, None, None, None),
        P("section", DP, None, None, None, None),
        P("section", DP, None, None, None, None),
        P("section", DP, None),
        P("section", DP, None),
        P("section", DP, None),
        P("section", None),
        P("section", None),
        P("section", None),
    )
    return jax.shard_map(
        shards,
        mesh=fine,
        in_specs=placed,
        out_specs=(
            P(DP, None),
            P("section", DP, None, None, None, None),
            P("section", DP, None),
            P("section", DP, None),
            P("section", DP, None),
        ),
        check_vma=False,
    )
```

```python
import functools

import jax
import jax.numpy as jnp
from jax import lax
from jax.experimental import pallas as pl
from jax.experimental.pallas import tpu as pltpu
from jax.sharding import Mesh
from jax.sharding import PartitionSpec as P

MICRO = 2
SOFTMAX_TEMP = 0.5
LOSS_SCALE = 1024.0
PLANE = ("x", "y", "core")
DP = ("z_hi", "x", "y", "core")
LANES = 128
TILE = 256
BF = jnp.bfloat16
F32 = jnp.float32
ROWS_BY_ROWS = (((1,), (1,)), ((), ()))
VMEM_LIMIT = 24 * 1024 * 1024


def three_parts(values):
    high = values.astype(BF)
    rest = values - high.astype(F32)
    middle = rest.astype(BF)
    return high, middle, (rest - middle.astype(F32)).astype(BF)


def prepare_kernel(
    where_ref,
    final_hbm,
    incoming_hbm,
    mid1_hbm,
    mid2_hbm,
    input_hbm,
    one_hbm,
    two_ref,
    in_hbm,
    base_ref,
    final_ref,
    mid1_ref,
    mid2_ref,
    input_ref,
    one_ref,
    in_ref,
    read_sems,
    write_sems,
):
    rows, narrow = mid1_ref.shape
    wide = input_ref.shape[1]
    crop_rows = rows // MICRO
    reads = [
        pltpu.make_async_copy(source, target, read_sems.at[place])
        for place, (source, target) in enumerate(
            ((mid1_hbm, mid1_ref), (mid2_hbm, mid2_ref), (input_hbm, input_ref))
        )
    ]
    for read in reads:
        read.start()
    write_one = pltpu.make_async_copy(one_ref, one_hbm, write_sems.at[0])
    write_in = pltpu.make_async_copy(in_ref, in_hbm, write_sems.at[1])
    empty = jnp.zeros((64, narrow), BF)
    reads[0].wait()
    for crop in range(MICRO):
        at = slice(crop * crop_rows, (crop + 1) * crop_rows)
        hidden = jnp.maximum(mid1_ref[at, :], 0)
        moved = (
            jnp.concatenate([empty, hidden[:-64]], axis=0),
            hidden,
            jnp.concatenate([hidden[64:], empty], axis=0),
        )
        for off_a in range(3):
            one_ref[off_a * narrow : (off_a + 1) * narrow, at] = moved[off_a].T
    write_one.start()
    reads[1].wait()
    two_ref[...] = jnp.maximum(mid2_ref[...], 0).T
    reads[2].wait()
    for part in range(wide // LANES):
        lanes = slice(part * LANES, (part + 1) * LANES)
        in_ref[lanes, :] = jnp.maximum(input_ref[:, lanes], 0).T
    write_in.start()

    @pl.when(where_ref[0] != 0)
    def _():
        read = pltpu.make_async_copy(final_hbm, final_ref, read_sems.at[3])
        read.start()
        read.wait()
        base_ref[...] = jnp.where(final_ref[...].astype(F32) > 0, 1.0, 0.0).astype(BF)

    @pl.when(where_ref[0] == 0)
    def _():
        read = pltpu.make_async_copy(incoming_hbm, base_ref, read_sems.at[3])
        read.start()
        read.wait()

    write_one.wait()
    write_in.wait()


def prepare_step(place, final, incoming, mid1, mid2, input_pre):
    rows, narrow = mid1.shape
    wide = input_pre.shape[1]
    smem = pl.BlockSpec(memory_space=pltpu.SMEM)
    hbm = pl.BlockSpec(memory_space=pltpu.HBM)
    vmem = pl.BlockSpec(memory_space=pltpu.VMEM)
    held = (final.shape, mid1.shape, mid2.shape, input_pre.shape)
    turned = ((3 * narrow, rows), (wide, rows))
    return pl.pallas_call(
        prepare_kernel,
        out_shape=(
            pltpu.HBM(turned[0], BF),
            pltpu.VMEM((narrow, rows), BF),
            pltpu.HBM(turned[1], BF),
            pltpu.VMEM((rows, wide), BF),
        ),
        in_specs=[smem] + [hbm] * 5,
        out_specs=(hbm, vmem, hbm, vmem),
        scratch_shapes=[pltpu.VMEM(shape, BF) for shape in (*held, *turned)]
        + [pltpu.SemaphoreType.DMA((4,)), pltpu.SemaphoreType.DMA((2,))],
        compiler_params=pltpu.CompilerParams(vmem_limit_bytes=VMEM_LIMIT),
        cost_estimate=pl.CostEstimate(flops=0, bytes_accessed=6_000_000, transcendentals=0),
        name="prepare",
    )(place, *in_hbm(final, incoming, mid1, mid2, input_pre))


def unpack_kernel(
    where_ref,
    near_ref,
    across_ref,
    spatial_ref,
    expand_ref,
    reduce_ref,
    spatial_rows,
    expand_rows,
    reduce_rows,
):
    narrow = near_ref.shape[1]
    chips = near_ref.shape[0] // 144

    def unpack(source, chip, core):
        shard = source[chip * 144 : (chip + 1) * 144, :].astype(F32)
        for half in range(2):
            device = half * 2 * chips + chip * 2 + core
            top = half * 72
            reduce_rows[device * 8 : device * 8 + 8, :] = shard[top : top + 8]
            for part in range(8):
                row, lane = device * 2 + part // 4, part % 4 * LANES
                expand_rows[row : row + 1, lane : lane + LANES] = shard[
                    top + 8 + part : top + 9 + part
                ]
            spatial_rows[device * 54 : device * 54 + 54, :] = shard[top + 16 : top + 70]

    for core in range(2):

        @pl.when(where_ref[1] == core)
        def _(core=core):
            for chip in range(chips):
                unpack(near_ref, chip, core)
                unpack(across_ref, chip, 1 - core)

    reduce_ref[...] = reduce_rows[...].astype(BF)
    expand_ref[...] = expand_rows[...].astype(BF)
    for off_a in range(3):
        for position in range(9):
            block = off_a * 9 + position
            spatial_ref[
                off_a * narrow : (off_a + 1) * narrow, position * narrow : (position + 1) * narrow
            ] = spatial_rows[block * narrow : (block + 1) * narrow, :].astype(BF)


def unpack_step(place, near, across, wide):
    narrow = near.shape[1]
    smem = pl.BlockSpec(memory_space=pltpu.SMEM)
    vmem = pl.BlockSpec(memory_space=pltpu.VMEM)
    outs = ((3 * narrow, 9 * narrow), (narrow, wide), (wide, narrow))
    return pl.pallas_call(
        unpack_kernel,
        out_shape=(
            pltpu.VMEM(outs[0], BF),
            pltpu.VMEM(outs[1], BF),
            jax.ShapeDtypeStruct(outs[2], BF),
        ),
        in_specs=[smem] + [vmem] * 2,
        out_specs=(vmem,) * 3,
        scratch_shapes=[
            pltpu.VMEM((27 * narrow, narrow), F32),
            pltpu.VMEM((narrow, wide), F32),
            pltpu.VMEM((wide, narrow), F32),
        ],
        compiler_params=pltpu.CompilerParams(vmem_limit_bytes=VMEM_LIMIT),
        cost_estimate=pl.CostEstimate(flops=0, bytes_accessed=3_000_000, transcendentals=0),
        name="unpack",
    )(place, *in_vmem(near, across))


def loss_kernel(
    where_ref,
    plan_ref,
    near_ref,
    across_ref,
    partner_ref,
    head_pre_ref,
    head_in_ref,
    head_out_ref,
    grad_ref,
    pool_ref,
    left,
    right,
    even,
    odd,
    totals,
):
    crops = left.shape[0]
    own = grad_ref.shape[0]
    tiles = crops // TILE
    first = pl.multiple_of(where_ref[0], own)

    for half, rows_ref in enumerate((near_ref, across_ref)):
        count = rows_ref.shape[0]

        def split(r, _, half=half, rows_ref=rows_ref, count=count):
            a, b, c = three_parts(rows_ref[pl.ds(pl.multiple_of(r * TILE, TILE), TILE), :])
            at = pl.ds(pl.multiple_of(half * count + r * TILE, TILE), TILE)
            a2, b2, c2 = a * 2, b * 2, c * 2
            for place, part in enumerate((a2, b2, a2, b2, a2, c2)):
                left[at, place * LANES : (place + 1) * LANES] = part
            for place, part in enumerate((a, a, b, b, c, a)):
                right[at, place * LANES : (place + 1) * LANES] = part
            return 0

        lax.fori_loop(0, count // TILE, split, 0)

    diagonal = lax.broadcasted_iota(jnp.int32, (TILE, TILE), 0) == lax.broadcasted_iota(
        jnp.int32, (TILE, TILE), 1
    )
    groups = crops // 8

    def score_block(j, scores):
        at = pl.ds(pl.multiple_of(j * TILE, TILE), TILE)
        scores[...] = lax.dot_general(
            left[...], right[at, :], ROWS_BY_ROWS, preferred_element_type=F32
        )
        scores[at, :] = jnp.where(diagonal, -jnp.inf, scores[at, :])
        largest = jnp.max(scores[...].reshape(groups, 8, TILE), axis=0)
        return jnp.broadcast_to(jnp.max(largest, axis=0, keepdims=True), (8, TILE))

    def sum_block(j, scores, largest):
        at = pl.ds(pl.multiple_of(j * TILE, TILE), TILE)
        summed = jnp.sum(jnp.exp(scores[...].reshape(groups, 8, TILE) - largest[None]), axis=0)
        whole = jnp.broadcast_to(jnp.sum(summed, axis=0, keepdims=True), (8, TILE))
        totals[:, at] = largest + jnp.log(whole)

    def two_blocks(pair, largest):
        j = 2 * pair
        following = score_block(j + 1, odd)
        sum_block(j, even, largest)
        after = score_block(j + 2, even)
        sum_block(j + 1, odd, following)
        return after

    largest = lax.fori_loop(0, tiles // 2 - 1, two_blocks, score_block(0, even))
    following = score_block(tiles - 1, odd)
    sum_block(tiles - 2, even, largest)
    sum_block(tiles - 1, odd, following)

    mine = lax.dot_general(
        left[pl.ds(first, own), :], right[...], ROWS_BY_ROWS, preferred_element_type=F32
    )
    columns = lax.broadcasted_iota(jnp.int32, (own, crops), 1)
    mine = jnp.where(
        columns == lax.broadcasted_iota(jnp.int32, (own, crops), 0) + first, -jnp.inf, mine
    )
    peak = jnp.max(mine, axis=1, keepdims=True)
    my_totals = peak + jnp.log(jnp.sum(jnp.exp(mine - peak), axis=1, keepdims=True))
    blended = jnp.exp(mine - my_totals) + jnp.exp(mine - totals[0:1, :])
    blended = blended - jnp.where(columns == partner_ref[...], 2.0, 0.0)
    a, b, c = three_parts(blended)
    stacked = jnp.concatenate([a, b, c], axis=0)
    products = jnp.dot(stacked, right[:, LANES : 3 * LANES], preferred_element_type=F32)
    low = jnp.dot(a, right[:, 4 * LANES : 5 * LANES], preferred_element_type=F32)
    small = products[own : 2 * own, LANES:] + products[2 * own :, :LANES] + low
    gradient = (
        products[:own, :LANES] + (products[:own, LANES:] + products[own : 2 * own, :LANES] + small)
    ) / SOFTMAX_TEMP
    grad_ref[...] = gradient

    pick_row = lax.broadcasted_iota(jnp.int32, (16, own), 0)
    pick_column = lax.broadcasted_iota(jnp.int32, (16, own), 1)
    wanted = jnp.where(pick_row == 0, plan_ref[0, 0], plan_ref[0, 1])
    chosen = jnp.where((pick_column == wanted) & (pick_row < MICRO), 1.0, 0.0).astype(BF)
    picked = jnp.dot(chosen, gradient.astype(BF), preferred_element_type=F32).astype(BF)
    hid_back = lax.dot_general(
        picked, head_out_ref[...], ROWS_BY_ROWS, preferred_element_type=F32
    )
    hid_grad = jnp.where(head_pre_ref[...].astype(F32) > 0, hid_back[:MICRO], 0.0)
    hid_grad = jnp.concatenate(
        [hid_grad, jnp.zeros((16 - MICRO, hid_grad.shape[1]), F32)], axis=0
    ).astype(BF)
    pool = lax.dot_general(hid_grad, head_in_ref[...], ROWS_BY_ROWS, preferred_element_type=F32)
    parts = pool.shape[1] // LANES
    packed = jnp.concatenate(
        [pool[m : m + 1, n * LANES : (n + 1) * LANES] for m in range(MICRO) for n in range(parts)],
        axis=0,
    )
    for copy in range(pool_ref.shape[0] // packed.shape[0]):
        pool_ref[copy * packed.shape[0] : (copy + 1) * packed.shape[0], :] = packed


def loss_step(first_row, plan, near, across, partner_row, head_pre, head_in, head_out, own, sections):
    crops, width = 2 * near.shape[0], near.shape[1]
    pool_rows = MICRO * head_in.shape[0] // LANES
    smem = pl.BlockSpec(memory_space=pltpu.SMEM)
    vmem = pl.BlockSpec(memory_space=pltpu.VMEM)
    return pl.pallas_call(
        loss_kernel,
        out_shape=(
            jax.ShapeDtypeStruct((own, width), F32),
            jax.ShapeDtypeStruct((sections * pool_rows, LANES), F32),
        ),
        in_specs=[smem, smem] + [vmem] * 6,
        out_specs=(vmem, vmem),
        scratch_shapes=[
            pltpu.VMEM((crops, 6 * LANES), BF),
            pltpu.VMEM((crops, 6 * LANES), BF),
            pltpu.VMEM((crops, TILE), F32),
            pltpu.VMEM((crops, TILE), F32),
            pltpu.VMEM((8, crops), F32),
        ],
        compiler_params=pltpu.CompilerParams(vmem_limit_bytes=VMEM_LIMIT),
        cost_estimate=pl.CostEstimate(
            flops=12_000_000_000, bytes_accessed=2_000_000, transcendentals=4_000_000
        ),
        name="loss",
    )(first_row, plan, *in_vmem(near, across), partner_row, head_pre, head_in, head_out)


def pooled_scale(last, pool_ref, voxels):
    rows = MICRO * 4
    total = pool_ref[0:rows, :]
    for source in range(1, pool_ref.shape[0] // rows):
        total = total + pool_ref[source * rows : (source + 1) * rows, :]
    return jnp.where(last, total * (LOSS_SCALE / voxels), 1.0)


def out_grad_tile(scale, crop, part, base):
    return base.astype(F32) * scale[crop * 4 + part : crop * 4 + part + 1, :]


def block_kernel(
    where_ref,
    pool_ref,
    base_ref,
    mid1_hbm,
    mid2_hbm,
    turned1_hbm,
    turned2_ref,
    turned_in_hbm,
    spatial_ref,
    expand_ref,
    gain1_ref,
    gain2_ref,
    gain3_ref,
    kept_ref,
    given_ref,
    e_one_ref,
    e_three,
    shifts,
    spatial_sum,
    expand_sum,
    reduce_sum,
    chunk,
    mid1_ref,
    mid2_ref,
    turned1_ref,
    turned_in_ref,
    read_sems,
):
    reads = [
        pltpu.make_async_copy(mid2_hbm, mid2_ref, read_sems.at[0]),
        pltpu.make_async_copy(mid1_hbm, mid1_ref, read_sems.at[1]),
        pltpu.make_async_copy(turned_in_hbm, turned_in_ref, read_sems.at[2]),
        pltpu.make_async_copy(turned1_hbm, turned1_ref, read_sems.at[3]),
    ]
    for read in reads:
        read.start()
    side = 8
    rows, narrow = mid1_ref.shape
    wide = e_three.shape[1]
    crop_rows = rows // MICRO
    plane = side * side
    inverse = 1.0 / (MICRO * 64)
    scale = pooled_scale(where_ref[0] != 0, pool_ref, side * plane)

    step = 256
    for start in range(0, rows, step):
        crop = start // crop_rows
        for part in range(wide // LANES):
            lanes = slice(part * LANES, (part + 1) * LANES)
            at = slice(start, start + step)
            out_grad = out_grad_tile(scale, crop, part, base_ref[at, lanes])
            e_three[at, lanes] = (gain3_ref[:, lanes] * out_grad).astype(BF)

    expand_sum[...] = jnp.dot(turned2_ref[...], e_three[...], preferred_element_type=F32) * inverse
    reads[0].wait()

    for start in range(0, rows, crop_rows):
        at = slice(start, start + crop_rows)
        back = lax.dot_general(
            e_three[at, :], expand_ref[...], ROWS_BY_ROWS, preferred_element_type=F32
        )
        e_two = jnp.where(mid2_ref[at, :].astype(F32) > 0, gain2_ref[...] * back, 0.0)
        e_two = e_two.astype(BF).astype(F32).reshape(plane, side, narrow)
        place = lax.broadcasted_iota(jnp.int32, e_two.shape, 1)
        none = jnp.zeros((side, 1, side, narrow), F32)
        for off_c in (-1, 0, 1):
            if off_c == 0:
                moved = e_two
            elif off_c == 1:
                moved = jnp.where(place == 0, 0.0, pltpu.roll(e_two, 1, 1))
            else:
                moved = jnp.where(place == side - 1, 0.0, pltpu.roll(e_two, side - 1, 1))
            moved = moved.reshape(side, side, side, narrow)
            for off_b in (-1, 0, 1):
                if off_b == 0:
                    both = moved
                elif off_b == 1:
                    both = jnp.concatenate([none, moved[:, :-1]], axis=1)
                else:
                    both = jnp.concatenate([moved[:, 1:], none], axis=1)
                position = 3 * (off_b + 1) + (off_c + 1)
                shifts[at, position * narrow : (position + 1) * narrow] = both.reshape(
                    crop_rows, narrow
                ).astype(BF)

    reads[1].wait()
    empty = jnp.zeros((plane, narrow), F32)
    for crop in range(MICRO):
        at = slice(crop * crop_rows, (crop + 1) * crop_rows)
        spread = lax.dot_general(
            shifts[at, :], spatial_ref[...], ROWS_BY_ROWS, preferred_element_type=F32
        )
        lower = jnp.concatenate([spread[plane:, :narrow], empty], axis=0)
        upper = jnp.concatenate([empty, spread[:-plane, 2 * narrow :]], axis=0)
        back_one = lower + spread[:, narrow : 2 * narrow] + upper
        e_one_ref[at, :] = jnp.where(
            mid1_ref[at, :].astype(F32) > 0, gain1_ref[...] * back_one, 0.0
        ).astype(BF)

    reads[2].wait()
    reduce_sum[...] = (
        jnp.dot(turned_in_ref[...], e_one_ref[...], preferred_element_type=F32) * inverse
    )

    reads[3].wait()
    for off_a in range(3):
        summed = (
            jnp.dot(
                turned1_ref[off_a * narrow : (off_a + 1) * narrow, :],
                shifts[...],
                preferred_element_type=F32,
            )
            * inverse
        )
        for position in range(9):
            block = off_a * 9 + position
            spatial_sum[block * narrow : (block + 1) * narrow, :] = summed[
                :, position * narrow : (position + 1) * narrow
            ]

    chips = 16
    height = kept_ref.shape[0] // chips
    chunk[140:144, :] = jnp.zeros((4, narrow), F32)

    def pack(chip, to, out_ref):
        for half in range(2):
            device = half * 2 * chips + chip * 2 + to
            chunk[half * 8 : half * 8 + 8, :] = reduce_sum[device * 8 : device * 8 + 8, :]
            for part in range(4):
                chunk[16 + half * 8 + part * 2 : 18 + half * 8 + part * 2, :] = expand_sum[
                    device * 2 : device * 2 + 2, part * LANES : (part + 1) * LANES
                ]
            chunk[32 + half * 54 : 86 + half * 54, :] = spatial_sum[
                device * 54 : device * 54 + 54, :
            ]
        out_ref[chip * height : (chip + 1) * height, :] = chunk[...].astype(BF)

    for core in range(2):

        @pl.when(where_ref[1] == core)
        def _(core=core):
            for chip in range(chips):
                pack(chip, core, kept_ref)
                pack(chip, 1 - core, given_ref)


def block_step(place, pool, base, mid1, mid2, turned1, turned2, turned_in, spatial, expand, gains):
    rows, narrow = mid1.shape
    wide = base.shape[1]
    smem = pl.BlockSpec(memory_space=pltpu.SMEM)
    vmem = pl.BlockSpec(memory_space=pltpu.VMEM)
    hbm = pl.BlockSpec(memory_space=pltpu.HBM)
    return pl.pallas_call(
        block_kernel,
        out_shape=(
            jax.ShapeDtypeStruct((16 * 144, narrow), BF),
            jax.ShapeDtypeStruct((16 * 144, narrow), BF),
            jax.ShapeDtypeStruct((rows, narrow), BF),
        ),
        in_specs=[smem, vmem, vmem, hbm, hbm, hbm, vmem, hbm] + [vmem] * 5,
        out_specs=(vmem, vmem, vmem),
        scratch_shapes=[
            pltpu.VMEM((rows, wide), BF),
            pltpu.VMEM((rows, 9 * narrow), BF),
            pltpu.VMEM((27 * narrow, narrow), F32),
            pltpu.VMEM((narrow, wide), F32),
            pltpu.VMEM((wide, narrow), F32),
            pltpu.VMEM((144, narrow), F32),
        ]
        + [pltpu.VMEM(array.shape, BF) for array in (mid1, mid2, turned1, turned_in)]
        + [pltpu.SemaphoreType.DMA((4,))],
        compiler_params=pltpu.CompilerParams(vmem_limit_bytes=VMEM_LIMIT),
        cost_estimate=pl.CostEstimate(
            flops=4_000_000_000, bytes_accessed=6_000_000, transcendentals=0
        ),
        name="block",
    )(
        place,
        pool,
        *in_vmem(base),
        *in_hbm(mid1, mid2, turned1),
        *in_vmem(turned2),
        *in_hbm(turned_in),
        *in_vmem(spatial, expand),
        *gains,
    )


def input_kernel(
    where_ref, pool_ref, base_ref, input_hbm, e_one_ref, reduce_ref, out_ref, input_ref, read_sem
):
    read = pltpu.make_async_copy(input_hbm, input_ref, read_sem.at[0])
    read.start()
    rows, wide = input_ref.shape
    crop_rows = rows // MICRO
    scale = pooled_scale(where_ref[0] != 0, pool_ref, crop_rows)
    read.wait()
    step = 256
    for start in range(0, rows, step):
        at = slice(start, start + step)
        through = lax.dot_general(
            e_one_ref[at, :], reduce_ref[...], ROWS_BY_ROWS, preferred_element_type=F32
        )
        for part in range(wide // LANES):
            lanes = slice(part * LANES, (part + 1) * LANES)
            out_grad = out_grad_tile(scale, start // crop_rows, part, base_ref[at, lanes])
            out_ref[at, lanes] = jnp.where(
                input_ref[at, lanes].astype(F32) > 0, through[:, lanes] + out_grad, 0.0
            ).astype(BF)


def input_step(place, pool, base, input_pre, e_one, reduce):
    smem = pl.BlockSpec(memory_space=pltpu.SMEM)
    vmem = pl.BlockSpec(memory_space=pltpu.VMEM)
    hbm = pl.BlockSpec(memory_space=pltpu.HBM)
    return pl.pallas_call(
        input_kernel,
        out_shape=jax.ShapeDtypeStruct(input_pre.shape, BF),
        in_specs=[smem, vmem, vmem, hbm, vmem, vmem],
        out_specs=vmem,
        scratch_shapes=[pltpu.VMEM(input_pre.shape, BF), pltpu.SemaphoreType.DMA((1,))],
        compiler_params=pltpu.CompilerParams(vmem_limit_bytes=VMEM_LIMIT),
        cost_estimate=pl.CostEstimate(
            flops=200_000_000, bytes_accessed=6_000_000, transcendentals=0
        ),
        name="input_grad",
    )(place, pool, base, *in_hbm(input_pre), e_one, reduce)


def sum_kernel(half_ref, shares_ref, kept_ref, given_ref, total, other):
    height = total.shape[0]
    summed = shares_ref[0:height, :].astype(F32)
    for source in range(1, shares_ref.shape[0] // height):
        summed = summed + shares_ref[source * height : (source + 1) * height, :].astype(F32)
    total[...] = summed
    other[72:80, :] = jnp.zeros((8, LANES), F32)

    def put(target, half):
        target[0:8, :] = total[half * 8 : half * 8 + 8, :]
        target[8:16, :] = total[16 + half * 8 : 24 + half * 8, :]
        target[16:72, :] = total[32 + half * 54 : 88 + half * 54, :]

    @pl.when(half_ref[0] == 0)
    def _():
        put(kept_ref, 0)
        put(other, 1)

    @pl.when(half_ref[0] != 0)
    def _():
        put(kept_ref, 1)
        put(other, 0)

    given_ref[...] = other[...].astype(BF)


def sum_step(half, shares):
    smem = pl.BlockSpec(memory_space=pltpu.SMEM)
    vmem = pl.BlockSpec(memory_space=pltpu.VMEM)
    return pl.pallas_call(
        sum_kernel,
        out_shape=(
            jax.ShapeDtypeStruct((72, LANES), F32),
            jax.ShapeDtypeStruct((80, LANES), BF),
        ),
        in_specs=[smem, vmem],
        out_specs=(vmem, vmem),
        scratch_shapes=[pltpu.VMEM((144, LANES), F32), pltpu.VMEM((80, LANES), F32)],
        compiler_params=pltpu.CompilerParams(vmem_limit_bytes=VMEM_LIMIT),
        name="shares",
    )(half, shares)


def last_kernel(kept_ref, got_ref, reduce_ref, spatial_ref, expand_ref):
    total = kept_ref[...] + got_ref[...].astype(F32)[0:72]
    reduce_ref[...] = total[0:8, :].astype(BF)
    spatial_ref[...] = total[16:70, :].astype(BF)
    expand_ref[...] = jnp.concatenate(
        [total[8 + 2 * part : 10 + 2 * part, :] for part in range(4)], axis=1
    ).astype(BF)


def last_step(kept, got):
    vmem = pl.BlockSpec(memory_space=pltpu.VMEM)
    return pl.pallas_call(
        last_kernel,
        out_shape=(
            jax.ShapeDtypeStruct((8, LANES), BF),
            jax.ShapeDtypeStruct((54, LANES), BF),
            jax.ShapeDtypeStruct((2, 4 * LANES), BF),
        ),
        in_specs=[vmem] * 2,
        out_specs=(vmem,) * 3,
        compiler_params=pltpu.CompilerParams(vmem_limit_bytes=2 * 1024 * 1024),
        name="weight_grads",
    )(kept, got)


def copies(shard, count):
    rows, width = shard.shape
    return jnp.broadcast_to(shard[None], (count, rows, width)).reshape(count * rows, width)


def in_vmem(*arrays):
    return [pltpu.with_memory_space_constraint(array, pltpu.VMEM) for array in arrays]


def in_hbm(*arrays):
    return [pltpu.with_memory_space_constraint(array, pltpu.HBM) for array in arrays]


def shards(
    projections,
    partner,
    plan,
    head_pre,
    head_in,
    head_out,
    final_pre,
    incoming,
    input_pre,
    mid_pre1,
    mid_pre2,
    w_reduce,
    w_spatial,
    w_expand,
    gain1,
    gain2,
    gain3,
):
    row_count = projections.shape[0]
    sections = lax.axis_size("section")
    peers = lax.axis_size(PLANE)
    upper = lax.axis_index("z_hi")
    me = lax.axis_index(PLANE)
    swap_near = [
        (half * sections + s, (1 - half) * sections + (s + sections // 2) % sections)
        for half in range(2)
        for s in range(sections)
    ]
    swap_far = [(0, 1), (1, 0)]
    narrow = w_reduce.shape[2]
    wide = w_expand.shape[2]
    core = lax.axis_index("core")
    section = lax.axis_index("section")
    chips = peers // 2
    other_rows = lax.ppermute(projections, ("z_hi", "section"), swap_near)
    n_reduce, n_spatial = w_reduce.shape[1], w_spatial.shape[1]
    n_expand = w_expand.shape[1] * wide // narrow
    packed = jnp.concatenate(
        [
            w_reduce[0],
            w_expand[0].reshape(n_expand, narrow),
            w_spatial[0],
            w_reduce[0, : 72 - n_reduce - n_expand - n_spatial],
        ],
        axis=0,
    )
    flat_one = mid_pre1.reshape(-1, narrow)
    flat_two = mid_pre2.reshape(-1, narrow)
    flat_in = input_pre.reshape(-1, wide)
    is_last = section == sections - 1
    place = jnp.stack([is_last.astype(jnp.int32), core.astype(jnp.int32)])
    sent, packed = lax.optimization_barrier(
        (copies(jnp.concatenate([projections, other_rows], axis=0), chips), packed)
    )
    near = lax.all_to_all(sent, ("x", "y"), 0, 0, tiled=True)
    far = lax.ppermute(packed, "z_hi", swap_far)
    ordered = jnp.where(
        upper == 0,
        jnp.concatenate([packed, far], axis=0),
        jnp.concatenate([far, packed], axis=0),
    )
    near, weights = lax.optimization_barrier((near, copies(ordered, chips)))
    across = lax.ppermute(near, "core", swap_far)
    half_crops = peers * row_count
    partner_device = partner % half_crops // row_count
    partner_row = (
        jnp.where(partner_device % 2 == core, 0, half_crops)
        + partner_device // 2 * (2 * row_count)
        + jnp.where(partner // half_crops == upper, 0, row_count)
        + partner % row_count
    )

    weights_near = lax.all_to_all(weights, ("x", "y"), 0, 0, tiled=True)
    projection_gradient, pool_copies = loss_step(
        (me // 2 * 2 * row_count).reshape(1),
        plan,
        near,
        across,
        partner_row.reshape(-1, 1),
        head_pre,
        head_in,
        head_out,
        row_count,
        sections,
    )
    pool = lax.all_to_all(pool_copies, "section", 0, 0, tiled=True)
    weights_near, pool_copies = lax.optimization_barrier((weights_near, pool_copies))
    weights_across = lax.ppermute(weights_near, "core", swap_far)
    place, weights_across = lax.optimization_barrier((place, weights_across))
    turned_one, turned_two, turned_in, base = prepare_step(
        place,
        final_pre.reshape(-1, wide),
        incoming.reshape(-1, wide),
        flat_one,
        flat_two,
        flat_in,
    )
    full_spatial, full_expand, full_reduce = unpack_step(
        place, weights_near, weights_across, wide
    )
    kept, given, e_one = block_step(
        place,
        pool,
        base,
        flat_one,
        flat_two,
        turned_one,
        turned_two,
        turned_in,
        full_spatial,
        full_expand,
        (gain1, gain2, gain3),
    )
    got = lax.ppermute(given, "core", swap_far)
    paired = (kept.astype(F32) + got.astype(F32)).astype(BF)
    shares = lax.all_to_all(paired, ("x", "y"), 0, 0, tiled=True)
    input_grad = input_step(place, pool, base, flat_in, e_one, full_reduce)
    kept, given = sum_step(upper.astype(jnp.int32).reshape(1), shares)
    got = lax.ppermute(given, "z_hi", swap_far)
    sum_reduce, sum_spatial, sum_expand = last_step(kept, got)
    return (
        projection_gradient,
        input_grad.reshape(input_pre.shape),
        sum_reduce[None],
        sum_spatial[None],
        sum_expand[None],
    )


def solution(mesh):
    fine = Mesh(
        mesh.devices.reshape(2, 4, 4, 2, mesh.shape["section"]),
        ("z_hi", "x", "y", "core", "section"),
    )
    placed = (
        P(DP, None),
        P(DP),
        P(DP, None),
        P(DP, "section"),
        P(None, "section"),
        P("section", None),
        P(DP, None, None, None, None),
        P("section", DP, None, None, None, None),
        P("section", DP, None, None, None, None),
        P("section", DP, None, None, None, None),
        P("section", DP, None, None, None, None),
        P("section", DP, None),
        P("section", DP, None),
        P("section", DP, None),
        P("section", None),
        P("section", None),
        P("section", None),
    )
    return jax.shard_map(
        shards,
        mesh=fine,
        in_specs=placed,
        out_specs=(
            P(DP, None),
            P("section", DP, None, None, None, None),
            P("section", DP, None),
            P("section", DP, None),
            P("section", DP, None),
        ),
        check_vma=False,
    )
```

```python
import functools

import jax
import jax.numpy as jnp
from jax import lax
from jax.experimental import pallas as pl
from jax.experimental.pallas import tpu as pltpu
from jax.sharding import Mesh
from jax.sharding import PartitionSpec as P

MICRO = 2
SOFTMAX_TEMP = 0.5
LOSS_SCALE = 1024.0
PLANE = ("x", "y", "core")
DP = ("z_hi", "x", "y", "core")
LANES = 128
TILE = 256
BF = jnp.bfloat16
F32 = jnp.float32
ROWS_BY_ROWS = (((1,), (1,)), ((), ()))
VMEM_LIMIT = 24 * 1024 * 1024


def three_parts(values):
    high = values.astype(BF)
    rest = values - high.astype(F32)
    middle = rest.astype(BF)
    return high, middle, (rest - middle.astype(F32)).astype(BF)


def prepare_kernel(
    where_ref,
    final_hbm,
    incoming_hbm,
    mid1_hbm,
    mid2_hbm,
    input_hbm,
    one_hbm,
    two_ref,
    in_hbm,
    base_ref,
    final_ref,
    mid1_ref,
    mid2_ref,
    input_ref,
    one_ref,
    in_ref,
    read_sems,
    write_sems,
):
    rows, narrow = mid1_ref.shape
    wide = input_ref.shape[1]
    crop_rows = rows // MICRO
    reads = [
        pltpu.make_async_copy(source, target, read_sems.at[place])
        for place, (source, target) in enumerate(
            ((mid1_hbm, mid1_ref), (mid2_hbm, mid2_ref), (input_hbm, input_ref))
        )
    ]
    for read in reads:
        read.start()
    write_one = pltpu.make_async_copy(one_ref, one_hbm, write_sems.at[0])
    write_in = pltpu.make_async_copy(in_ref, in_hbm, write_sems.at[1])
    empty = jnp.zeros((64, narrow), BF)
    reads[0].wait()
    for crop in range(MICRO):
        at = slice(crop * crop_rows, (crop + 1) * crop_rows)
        hidden = jnp.maximum(mid1_ref[at, :], 0)
        moved = (
            jnp.concatenate([empty, hidden[:-64]], axis=0),
            hidden,
            jnp.concatenate([hidden[64:], empty], axis=0),
        )
        for off_a in range(3):
            one_ref[off_a * narrow : (off_a + 1) * narrow, at] = moved[off_a].T
    write_one.start()
    reads[1].wait()
    two_ref[...] = jnp.maximum(mid2_ref[...], 0).T
    reads[2].wait()
    for part in range(wide // LANES):
        lanes = slice(part * LANES, (part + 1) * LANES)
        in_ref[lanes, :] = jnp.maximum(input_ref[:, lanes], 0).T
    write_in.start()

    @pl.when(where_ref[0] != 0)
    def _():
        read = pltpu.make_async_copy(final_hbm, final_ref, read_sems.at[3])
        read.start()
        read.wait()
        base_ref[...] = jnp.where(final_ref[...].astype(F32) > 0, 1.0, 0.0).astype(BF)

    @pl.when(where_ref[0] == 0)
    def _():
        read = pltpu.make_async_copy(incoming_hbm, base_ref, read_sems.at[3])
        read.start()
        read.wait()

    write_one.wait()
    write_in.wait()


def prepare_step(place, final, incoming, mid1, mid2, input_pre):
    rows, narrow = mid1.shape
    wide = input_pre.shape[1]
    smem = pl.BlockSpec(memory_space=pltpu.SMEM)
    hbm = pl.BlockSpec(memory_space=pltpu.HBM)
    vmem = pl.BlockSpec(memory_space=pltpu.VMEM)
    held = (final.shape, mid1.shape, mid2.shape, input_pre.shape)
    turned = ((3 * narrow, rows), (wide, rows))
    return pl.pallas_call(
        prepare_kernel,
        out_shape=(
            pltpu.HBM(turned[0], BF),
            pltpu.VMEM((narrow, rows), BF),
            pltpu.HBM(turned[1], BF),
            pltpu.VMEM((rows, wide), BF),
        ),
        in_specs=[smem] + [hbm] * 5,
        out_specs=(hbm, vmem, hbm, vmem),
        scratch_shapes=[pltpu.VMEM(shape, BF) for shape in (*held, *turned)]
        + [pltpu.SemaphoreType.DMA((4,)), pltpu.SemaphoreType.DMA((2,))],
        compiler_params=pltpu.CompilerParams(vmem_limit_bytes=VMEM_LIMIT),
        cost_estimate=pl.CostEstimate(flops=0, bytes_accessed=6_000_000, transcendentals=0),
        name="prepare",
    )(place, *in_hbm(final, incoming, mid1, mid2, input_pre))


def unpack_kernel(
    where_ref,
    near_ref,
    across_ref,
    spatial_ref,
    expand_ref,
    reduce_ref,
    spatial_rows,
    expand_rows,
    reduce_rows,
):
    narrow = near_ref.shape[1]
    chips = near_ref.shape[0] // 144

    def unpack(source, chip, core):
        shard = source[chip * 144 : (chip + 1) * 144, :].astype(F32)
        for half in range(2):
            device = half * 2 * chips + chip * 2 + core
            top = half * 72
            reduce_rows[device * 8 : device * 8 + 8, :] = shard[top : top + 8]
            for part in range(8):
                row, lane = device * 2 + part // 4, part % 4 * LANES
                expand_rows[row : row + 1, lane : lane + LANES] = shard[
                    top + 8 + part : top + 9 + part
                ]
            spatial_rows[device * 54 : device * 54 + 54, :] = shard[top + 16 : top + 70]

    for core in range(2):

        @pl.when(where_ref[1] == core)
        def _(core=core):
            for chip in range(chips):
                unpack(near_ref, chip, core)
                unpack(across_ref, chip, 1 - core)

    reduce_ref[...] = reduce_rows[...].astype(BF)
    expand_ref[...] = expand_rows[...].astype(BF)
    for off_a in range(3):
        for position in range(9):
            block = off_a * 9 + position
            spatial_ref[
                off_a * narrow : (off_a + 1) * narrow, position * narrow : (position + 1) * narrow
            ] = spatial_rows[block * narrow : (block + 1) * narrow, :].astype(BF)


def unpack_step(place, near, across, wide):
    narrow = near.shape[1]
    smem = pl.BlockSpec(memory_space=pltpu.SMEM)
    vmem = pl.BlockSpec(memory_space=pltpu.VMEM)
    outs = ((3 * narrow, 9 * narrow), (narrow, wide), (wide, narrow))
    return pl.pallas_call(
        unpack_kernel,
        out_shape=(
            pltpu.VMEM(outs[0], BF),
            pltpu.VMEM(outs[1], BF),
            jax.ShapeDtypeStruct(outs[2], BF),
        ),
        in_specs=[smem] + [vmem] * 2,
        out_specs=(vmem,) * 3,
        scratch_shapes=[
            pltpu.VMEM((27 * narrow, narrow), F32),
            pltpu.VMEM((narrow, wide), F32),
            pltpu.VMEM((wide, narrow), F32),
        ],
        compiler_params=pltpu.CompilerParams(vmem_limit_bytes=VMEM_LIMIT),
        cost_estimate=pl.CostEstimate(flops=0, bytes_accessed=3_000_000, transcendentals=0),
        name="unpack",
    )(place, *in_vmem(near, across))


def loss_kernel(
    where_ref,
    plan_ref,
    near_ref,
    across_ref,
    partner_ref,
    head_pre_ref,
    head_in_ref,
    head_out_ref,
    grad_ref,
    pool_ref,
    left,
    right,
    even,
    odd,
    totals,
):
    crops = left.shape[0]
    own = grad_ref.shape[0]
    tiles = crops // TILE
    first = pl.multiple_of(where_ref[0], own)

    for half, rows_ref in enumerate((near_ref, across_ref)):
        count = rows_ref.shape[0]

        def split(r, _, half=half, rows_ref=rows_ref, count=count):
            a, b, c = three_parts(rows_ref[pl.ds(pl.multiple_of(r * TILE, TILE), TILE), :])
            at = pl.ds(pl.multiple_of(half * count + r * TILE, TILE), TILE)
            a2, b2, c2 = a * 2, b * 2, c * 2
            for place, part in enumerate((a2, b2, a2, b2, a2, c2)):
                left[at, place * LANES : (place + 1) * LANES] = part
            for place, part in enumerate((a, a, b, b, c, a)):
                right[at, place * LANES : (place + 1) * LANES] = part
            return 0

        lax.fori_loop(0, count // TILE, split, 0)

    diagonal = lax.broadcasted_iota(jnp.int32, (TILE, TILE), 0) == lax.broadcasted_iota(
        jnp.int32, (TILE, TILE), 1
    )
    groups = crops // 8

    def score_block(j, scores):
        at = pl.ds(pl.multiple_of(j * TILE, TILE), TILE)
        scores[...] = lax.dot_general(
            left[...], right[at, :], ROWS_BY_ROWS, preferred_element_type=F32
        )
        scores[at, :] = jnp.where(diagonal, -jnp.inf, scores[at, :])
        largest = jnp.max(scores[...].reshape(groups, 8, TILE), axis=0)
        return jnp.broadcast_to(jnp.max(largest, axis=0, keepdims=True), (8, TILE))

    def sum_block(j, scores, largest):
        at = pl.ds(pl.multiple_of(j * TILE, TILE), TILE)
        summed = jnp.sum(jnp.exp(scores[...].reshape(groups, 8, TILE) - largest[None]), axis=0)
        whole = jnp.broadcast_to(jnp.sum(summed, axis=0, keepdims=True), (8, TILE))
        totals[:, at] = largest + jnp.log(whole)

    def two_blocks(pair, largest):
        j = 2 * pair
        following = score_block(j + 1, odd)
        sum_block(j, even, largest)
        after = score_block(j + 2, even)
        sum_block(j + 1, odd, following)
        return after

    largest = lax.fori_loop(0, tiles // 2 - 1, two_blocks, score_block(0, even))
    following = score_block(tiles - 1, odd)
    sum_block(tiles - 2, even, largest)
    sum_block(tiles - 1, odd, following)

    mine = lax.dot_general(
        left[pl.ds(first, own), :], right[...], ROWS_BY_ROWS, preferred_element_type=F32
    )
    columns = lax.broadcasted_iota(jnp.int32, (own, crops), 1)
    mine = jnp.where(
        columns == lax.broadcasted_iota(jnp.int32, (own, crops), 0) + first, -jnp.inf, mine
    )
    peak = jnp.max(mine, axis=1, keepdims=True)
    my_totals = peak + jnp.log(jnp.sum(jnp.exp(mine - peak), axis=1, keepdims=True))
    blended = jnp.exp(mine - my_totals) + jnp.exp(mine - totals[0:1, :])
    blended = blended - jnp.where(columns == partner_ref[...], 2.0, 0.0)
    a, b, c = three_parts(blended)
    stacked = jnp.concatenate([a, b, c], axis=0)
    products = jnp.dot(stacked, right[:, LANES : 3 * LANES], preferred_element_type=F32)
    low = jnp.dot(a, right[:, 4 * LANES : 5 * LANES], preferred_element_type=F32)
    small = products[own : 2 * own, LANES:] + products[2 * own :, :LANES] + low
    gradient = (
        products[:own, :LANES] + (products[:own, LANES:] + products[own : 2 * own, :LANES] + small)
    ) / SOFTMAX_TEMP
    grad_ref[...] = gradient

    pick_row = lax.broadcasted_iota(jnp.int32, (16, own), 0)
    pick_column = lax.broadcasted_iota(jnp.int32, (16, own), 1)
    wanted = jnp.where(pick_row == 0, plan_ref[0, 0], plan_ref[0, 1])
    chosen = jnp.where((pick_column == wanted) & (pick_row < MICRO), 1.0, 0.0).astype(BF)
    picked = jnp.dot(chosen, gradient.astype(BF), preferred_element_type=F32).astype(BF)
    hid_back = lax.dot_general(
        picked, head_out_ref[...], ROWS_BY_ROWS, preferred_element_type=F32
    )
    hid_grad = jnp.where(head_pre_ref[...].astype(F32) > 0, hid_back[:MICRO], 0.0)
    hid_grad = jnp.concatenate(
        [hid_grad, jnp.zeros((16 - MICRO, hid_grad.shape[1]), F32)], axis=0
    ).astype(BF)
    pool = lax.dot_general(hid_grad, head_in_ref[...], ROWS_BY_ROWS, preferred_element_type=F32)
    parts = pool.shape[1] // LANES
    packed = jnp.concatenate(
        [pool[m : m + 1, n * LANES : (n + 1) * LANES] for m in range(MICRO) for n in range(parts)],
        axis=0,
    )
    for copy in range(pool_ref.shape[0] // packed.shape[0]):
        pool_ref[copy * packed.shape[0] : (copy + 1) * packed.shape[0], :] = packed


def loss_step(first_row, plan, near, across, partner_row, head_pre, head_in, head_out, own, sections):
    crops, width = 2 * near.shape[0], near.shape[1]
    pool_rows = MICRO * head_in.shape[0] // LANES
    smem = pl.BlockSpec(memory_space=pltpu.SMEM)
    vmem = pl.BlockSpec(memory_space=pltpu.VMEM)
    return pl.pallas_call(
        loss_kernel,
        out_shape=(
            jax.ShapeDtypeStruct((own, width), F32),
            jax.ShapeDtypeStruct((sections * pool_rows, LANES), F32),
        ),
        in_specs=[smem, smem] + [vmem] * 6,
        out_specs=(vmem, vmem),
        scratch_shapes=[
            pltpu.VMEM((crops, 6 * LANES), BF),
            pltpu.VMEM((crops, 6 * LANES), BF),
            pltpu.VMEM((crops, TILE), F32),
            pltpu.VMEM((crops, TILE), F32),
            pltpu.VMEM((8, crops), F32),
        ],
        compiler_params=pltpu.CompilerParams(vmem_limit_bytes=VMEM_LIMIT),
        cost_estimate=pl.CostEstimate(
            flops=12_000_000_000, bytes_accessed=2_000_000, transcendentals=4_000_000
        ),
        name="loss",
    )(first_row, plan, *in_vmem(near, across), partner_row, head_pre, head_in, head_out)


def pooled_scale(last, pool_ref, voxels):
    rows = MICRO * 4
    total = pool_ref[0:rows, :]
    for source in range(1, pool_ref.shape[0] // rows):
        total = total + pool_ref[source * rows : (source + 1) * rows, :]
    return jnp.where(last, total * (LOSS_SCALE / voxels), 1.0)


def out_grad_tile(scale, crop, part, base):
    return base.astype(F32) * scale[crop * 4 + part : crop * 4 + part + 1, :]


def block_kernel(
    where_ref,
    pool_ref,
    base_ref,
    mid1_hbm,
    mid2_hbm,
    turned1_hbm,
    turned2_ref,
    turned_in_hbm,
    spatial_ref,
    expand_ref,
    gain1_ref,
    gain2_ref,
    gain3_ref,
    kept_ref,
    given_ref,
    e_one_ref,
    e_three,
    shifts,
    spatial_sum,
    expand_sum,
    reduce_sum,
    chunk,
    mid1_ref,
    mid2_ref,
    turned1_ref,
    turned_in_ref,
    read_sems,
):
    reads = [
        pltpu.make_async_copy(mid2_hbm, mid2_ref, read_sems.at[0]),
        pltpu.make_async_copy(mid1_hbm, mid1_ref, read_sems.at[1]),
        pltpu.make_async_copy(turned1_hbm, turned1_ref, read_sems.at[2]),
        pltpu.make_async_copy(turned_in_hbm, turned_in_ref, read_sems.at[3]),
    ]
    for read in reads:
        read.start()
    side = 8
    rows, narrow = mid1_ref.shape
    wide = e_three.shape[1]
    crop_rows = rows // MICRO
    plane = side * side
    inverse = 1.0 / (MICRO * 64)
    scale = pooled_scale(where_ref[0] != 0, pool_ref, side * plane)

    step = 256
    for start in range(0, rows, step):
        crop = start // crop_rows
        for part in range(wide // LANES):
            lanes = slice(part * LANES, (part + 1) * LANES)
            at = slice(start, start + step)
            out_grad = out_grad_tile(scale, crop, part, base_ref[at, lanes])
            e_three[at, lanes] = (gain3_ref[:, lanes] * out_grad).astype(BF)

    expand_sum[...] = jnp.dot(turned2_ref[...], e_three[...], preferred_element_type=F32) * inverse
    reads[0].wait()

    for start in range(0, rows, crop_rows):
        at = slice(start, start + crop_rows)
        back = lax.dot_general(
            e_three[at, :], expand_ref[...], ROWS_BY_ROWS, preferred_element_type=F32
        )
        e_two = jnp.where(mid2_ref[at, :].astype(F32) > 0, gain2_ref[...] * back, 0.0)
        e_two = e_two.astype(BF).astype(F32).reshape(plane, side, narrow)
        place = lax.broadcasted_iota(jnp.int32, e_two.shape, 1)
        none = jnp.zeros((side, 1, side, narrow), F32)
        for off_c in (-1, 0, 1):
            if off_c == 0:
                moved = e_two
            elif off_c == 1:
                moved = jnp.where(place == 0, 0.0, pltpu.roll(e_two, 1, 1))
            else:
                moved = jnp.where(place == side - 1, 0.0, pltpu.roll(e_two, side - 1, 1))
            moved = moved.reshape(side, side, side, narrow)
            for off_b in (-1, 0, 1):
                if off_b == 0:
                    both = moved
                elif off_b == 1:
                    both = jnp.concatenate([none, moved[:, :-1]], axis=1)
                else:
                    both = jnp.concatenate([moved[:, 1:], none], axis=1)
                position = 3 * (off_b + 1) + (off_c + 1)
                shifts[at, position * narrow : (position + 1) * narrow] = both.reshape(
                    crop_rows, narrow
                ).astype(BF)

    reads[1].wait()
    empty = jnp.zeros((plane, narrow), F32)
    for crop in range(MICRO):
        at = slice(crop * crop_rows, (crop + 1) * crop_rows)
        spread = lax.dot_general(
            shifts[at, :], spatial_ref[...], ROWS_BY_ROWS, preferred_element_type=F32
        )
        lower = jnp.concatenate([spread[plane:, :narrow], empty], axis=0)
        upper = jnp.concatenate([empty, spread[:-plane, 2 * narrow :]], axis=0)
        back_one = lower + spread[:, narrow : 2 * narrow] + upper
        e_one_ref[at, :] = jnp.where(
            mid1_ref[at, :].astype(F32) > 0, gain1_ref[...] * back_one, 0.0
        ).astype(BF)

    reads[2].wait()
    for off_a in range(3):
        summed = (
            jnp.dot(
                turned1_ref[off_a * narrow : (off_a + 1) * narrow, :],
                shifts[...],
                preferred_element_type=F32,
            )
            * inverse
        )
        for position in range(9):
            block = off_a * 9 + position
            spatial_sum[block * narrow : (block + 1) * narrow, :] = summed[
                :, position * narrow : (position + 1) * narrow
            ]

    reads[3].wait()
    reduce_sum[...] = (
        jnp.dot(turned_in_ref[...], e_one_ref[...], preferred_element_type=F32) * inverse
    )

    chips = 16
    height = kept_ref.shape[0] // chips
    chunk[140:144, :] = jnp.zeros((4, narrow), F32)

    def pack(chip, to, out_ref):
        for half in range(2):
            device = half * 2 * chips + chip * 2 + to
            chunk[half * 8 : half * 8 + 8, :] = reduce_sum[device * 8 : device * 8 + 8, :]
            for part in range(4):
                chunk[16 + half * 8 + part * 2 : 18 + half * 8 + part * 2, :] = expand_sum[
                    device * 2 : device * 2 + 2, part * LANES : (part + 1) * LANES
                ]
            chunk[32 + half * 54 : 86 + half * 54, :] = spatial_sum[
                device * 54 : device * 54 + 54, :
            ]
        out_ref[chip * height : (chip + 1) * height, :] = chunk[...].astype(BF)

    for core in range(2):

        @pl.when(where_ref[1] == core)
        def _(core=core):
            for chip in range(chips):
                pack(chip, core, kept_ref)
                pack(chip, 1 - core, given_ref)


def block_step(place, pool, base, mid1, mid2, turned1, turned2, turned_in, spatial, expand, gains):
    rows, narrow = mid1.shape
    wide = base.shape[1]
    smem = pl.BlockSpec(memory_space=pltpu.SMEM)
    vmem = pl.BlockSpec(memory_space=pltpu.VMEM)
    hbm = pl.BlockSpec(memory_space=pltpu.HBM)
    return pl.pallas_call(
        block_kernel,
        out_shape=(
            jax.ShapeDtypeStruct((16 * 144, narrow), BF),
            jax.ShapeDtypeStruct((16 * 144, narrow), BF),
            jax.ShapeDtypeStruct((rows, narrow), BF),
        ),
        in_specs=[smem, vmem, vmem, hbm, hbm, hbm, vmem, hbm] + [vmem] * 5,
        out_specs=(vmem, vmem, vmem),
        scratch_shapes=[
            pltpu.VMEM((rows, wide), BF),
            pltpu.VMEM((rows, 9 * narrow), BF),
            pltpu.VMEM((27 * narrow, narrow), F32),
            pltpu.VMEM((narrow, wide), F32),
            pltpu.VMEM((wide, narrow), F32),
            pltpu.VMEM((144, narrow), F32),
        ]
        + [pltpu.VMEM(array.shape, BF) for array in (mid1, mid2, turned1, turned_in)]
        + [pltpu.SemaphoreType.DMA((4,))],
        compiler_params=pltpu.CompilerParams(vmem_limit_bytes=VMEM_LIMIT),
        cost_estimate=pl.CostEstimate(
            flops=4_000_000_000, bytes_accessed=6_000_000, transcendentals=0
        ),
        name="block",
    )(
        place,
        pool,
        *in_vmem(base),
        *in_hbm(mid1, mid2, turned1),
        *in_vmem(turned2),
        *in_hbm(turned_in),
        *in_vmem(spatial, expand),
        *gains,
    )


def input_kernel(
    where_ref, pool_ref, base_ref, input_hbm, e_one_ref, reduce_ref, out_ref, input_ref, read_sem
):
    read = pltpu.make_async_copy(input_hbm, input_ref, read_sem.at[0])
    read.start()
    rows, wide = input_ref.shape
    crop_rows = rows // MICRO
    scale = pooled_scale(where_ref[0] != 0, pool_ref, crop_rows)
    read.wait()
    step = 256
    for start in range(0, rows, step):
        at = slice(start, start + step)
        through = lax.dot_general(
            e_one_ref[at, :], reduce_ref[...], ROWS_BY_ROWS, preferred_element_type=F32
        )
        for part in range(wide // LANES):
            lanes = slice(part * LANES, (part + 1) * LANES)
            out_grad = out_grad_tile(scale, start // crop_rows, part, base_ref[at, lanes])
            out_ref[at, lanes] = jnp.where(
                input_ref[at, lanes].astype(F32) > 0, through[:, lanes] + out_grad, 0.0
            ).astype(BF)


def input_step(place, pool, base, input_pre, e_one, reduce):
    smem = pl.BlockSpec(memory_space=pltpu.SMEM)
    vmem = pl.BlockSpec(memory_space=pltpu.VMEM)
    hbm = pl.BlockSpec(memory_space=pltpu.HBM)
    return pl.pallas_call(
        input_kernel,
        out_shape=jax.ShapeDtypeStruct(input_pre.shape, BF),
        in_specs=[smem, vmem, vmem, hbm, vmem, vmem],
        out_specs=vmem,
        scratch_shapes=[pltpu.VMEM(input_pre.shape, BF), pltpu.SemaphoreType.DMA((1,))],
        compiler_params=pltpu.CompilerParams(vmem_limit_bytes=VMEM_LIMIT),
        cost_estimate=pl.CostEstimate(
            flops=200_000_000, bytes_accessed=6_000_000, transcendentals=0
        ),
        name="input_grad",
    )(place, pool, base, *in_hbm(input_pre), e_one, reduce)


def sum_kernel(half_ref, shares_ref, kept_ref, given_ref, total, other):
    height = total.shape[0]
    summed = shares_ref[0:height, :].astype(F32)
    for source in range(1, shares_ref.shape[0] // height):
        summed = summed + shares_ref[source * height : (source + 1) * height, :].astype(F32)
    total[...] = summed
    other[72:80, :] = jnp.zeros((8, LANES), F32)

    def put(target, half):
        target[0:8, :] = total[half * 8 : half * 8 + 8, :]
        target[8:16, :] = total[16 + half * 8 : 24 + half * 8, :]
        target[16:72, :] = total[32 + half * 54 : 88 + half * 54, :]

    @pl.when(half_ref[0] == 0)
    def _():
        put(kept_ref, 0)
        put(other, 1)

    @pl.when(half_ref[0] != 0)
    def _():
        put(kept_ref, 1)
        put(other, 0)

    given_ref[...] = other[...].astype(BF)


def sum_step(half, shares):
    smem = pl.BlockSpec(memory_space=pltpu.SMEM)
    vmem = pl.BlockSpec(memory_space=pltpu.VMEM)
    return pl.pallas_call(
        sum_kernel,
        out_shape=(
            jax.ShapeDtypeStruct((72, LANES), F32),
            jax.ShapeDtypeStruct((80, LANES), BF),
        ),
        in_specs=[smem, vmem],
        out_specs=(vmem, vmem),
        scratch_shapes=[pltpu.VMEM((144, LANES), F32), pltpu.VMEM((80, LANES), F32)],
        compiler_params=pltpu.CompilerParams(vmem_limit_bytes=VMEM_LIMIT),
        name="shares",
    )(half, shares)


def last_kernel(kept_ref, got_ref, reduce_ref, spatial_ref, expand_ref):
    total = kept_ref[...] + got_ref[...].astype(F32)[0:72]
    reduce_ref[...] = total[0:8, :].astype(BF)
    spatial_ref[...] = total[16:70, :].astype(BF)
    expand_ref[...] = jnp.concatenate(
        [total[8 + 2 * part : 10 + 2 * part, :] for part in range(4)], axis=1
    ).astype(BF)


def last_step(kept, got):
    vmem = pl.BlockSpec(memory_space=pltpu.VMEM)
    return pl.pallas_call(
        last_kernel,
        out_shape=(
            jax.ShapeDtypeStruct((8, LANES), BF),
            jax.ShapeDtypeStruct((54, LANES), BF),
            jax.ShapeDtypeStruct((2, 4 * LANES), BF),
        ),
        in_specs=[vmem] * 2,
        out_specs=(vmem,) * 3,
        compiler_params=pltpu.CompilerParams(vmem_limit_bytes=2 * 1024 * 1024),
        name="weight_grads",
    )(kept, got)


def copies(shard, count):
    rows, width = shard.shape
    return jnp.broadcast_to(shard[None], (count, rows, width)).reshape(count * rows, width)


def in_vmem(*arrays):
    return [pltpu.with_memory_space_constraint(array, pltpu.VMEM) for array in arrays]


def in_hbm(*arrays):
    return [pltpu.with_memory_space_constraint(array, pltpu.HBM) for array in arrays]


def shards(
    projections,
    partner,
    plan,
    head_pre,
    head_in,
    head_out,
    final_pre,
    incoming,
    input_pre,
    mid_pre1,
    mid_pre2,
    w_reduce,
    w_spatial,
    w_expand,
    gain1,
    gain2,
    gain3,
):
    row_count = projections.shape[0]
    sections = lax.axis_size("section")
    peers = lax.axis_size(PLANE)
    upper = lax.axis_index("z_hi")
    me = lax.axis_index(PLANE)
    swap_near = [
        (half * sections + s, (1 - half) * sections + (s + sections // 2) % sections)
        for half in range(2)
        for s in range(sections)
    ]
    swap_far = [(0, 1), (1, 0)]
    narrow = w_reduce.shape[2]
    wide = w_expand.shape[2]
    core = lax.axis_index("core")
    section = lax.axis_index("section")
    chips = peers // 2
    other_rows = lax.ppermute(projections, ("z_hi", "section"), swap_near)
    n_reduce, n_spatial = w_reduce.shape[1], w_spatial.shape[1]
    n_expand = w_expand.shape[1] * wide // narrow
    packed = jnp.concatenate(
        [
            w_reduce[0],
            w_expand[0].reshape(n_expand, narrow),
            w_spatial[0],
            w_reduce[0, : 72 - n_reduce - n_expand - n_spatial],
        ],
        axis=0,
    )
    flat_one = mid_pre1.reshape(-1, narrow)
    flat_two = mid_pre2.reshape(-1, narrow)
    flat_in = input_pre.reshape(-1, wide)
    is_last = section == sections - 1
    place = jnp.stack([is_last.astype(jnp.int32), core.astype(jnp.int32)])
    sent, packed = lax.optimization_barrier(
        (copies(jnp.concatenate([projections, other_rows], axis=0), chips), packed)
    )
    near = lax.all_to_all(sent, ("x", "y"), 0, 0, tiled=True)
    far = lax.ppermute(packed, "z_hi", swap_far)
    ordered = jnp.where(
        upper == 0,
        jnp.concatenate([packed, far], axis=0),
        jnp.concatenate([far, packed], axis=0),
    )
    near, weights = lax.optimization_barrier((near, copies(ordered, chips)))
    across = lax.ppermute(near, "core", swap_far)
    half_crops = peers * row_count
    partner_device = partner % half_crops // row_count
    partner_row = (
        jnp.where(partner_device % 2 == core, 0, half_crops)
        + partner_device // 2 * (2 * row_count)
        + jnp.where(partner // half_crops == upper, 0, row_count)
        + partner % row_count
    )

    weights_near = lax.all_to_all(weights, ("x", "y"), 0, 0, tiled=True)
    projection_gradient, pool_copies = loss_step(
        (me // 2 * 2 * row_count).reshape(1),
        plan,
        near,
        across,
        partner_row.reshape(-1, 1),
        head_pre,
        head_in,
        head_out,
        row_count,
        sections,
    )
    pool = lax.all_to_all(pool_copies, "section", 0, 0, tiled=True)
    weights_near, pool_copies = lax.optimization_barrier((weights_near, pool_copies))
    weights_across = lax.ppermute(weights_near, "core", swap_far)
    place, weights_across = lax.optimization_barrier((place, weights_across))
    turned_one, turned_two, turned_in, base = prepare_step(
        place,
        final_pre.reshape(-1, wide),
        incoming.reshape(-1, wide),
        flat_one,
        flat_two,
        flat_in,
    )
    full_spatial, full_expand, full_reduce = unpack_step(
        place, weights_near, weights_across, wide
    )
    kept, given, e_one = block_step(
        place,
        pool,
        base,
        flat_one,
        flat_two,
        turned_one,
        turned_two,
        turned_in,
        full_spatial,
        full_expand,
        (gain1, gain2, gain3),
    )
    got = lax.ppermute(given, "core", swap_far)
    paired = (kept.astype(F32) + got.astype(F32)).astype(BF)
    shares = lax.all_to_all(paired, ("x", "y"), 0, 0, tiled=True)
    input_grad = input_step(place, pool, base, flat_in, e_one, full_reduce)
    kept, given = sum_step(upper.astype(jnp.int32).reshape(1), shares)
    got = lax.ppermute(given, "z_hi", swap_far)
    sum_reduce, sum_spatial, sum_expand = last_step(kept, got)
    return (
        projection_gradient,
        input_grad.reshape(input_pre.shape),
        sum_reduce[None],
        sum_spatial[None],
        sum_expand[None],
    )


def solution(mesh):
    fine = Mesh(
        mesh.devices.reshape(2, 4, 4, 2, mesh.shape["section"]),
        ("z_hi", "x", "y", "core", "section"),
    )
    placed = (
        P(DP, None),
        P(DP),
        P(DP, None),
        P(DP, "section"),
        P(None, "section"),
        P("section", None),
        P(DP, None, None, None, None),
        P("section", DP, None, None, None, None),
        P("section", DP, None, None, None, None),
        P("section", DP, None, None, None, None),
        P("section", DP, None, None, None, None),
        P("section", DP, None),
        P("section", DP, None),
        P("section", DP, None),
        P("section", None),
        P("section", None),
        P("section", None),
    )
    return jax.shard_map(
        shards,
        mesh=fine,
        in_specs=placed,
        out_specs=(
            P(DP, None),
            P("section", DP, None, None, None, None),
            P("section", DP, None),
            P("section", DP, None),
            P("section", DP, None),
        ),
        check_vma=False,
    )
```
